32 devices in a mesh: dom: 16 (over z, y, x), rep: 2 (over core).
Axes of the slice: x: 2, y: 2, z: 4, core: 2. Of those that a mesh axis runs over, the one named last changes fastest.
Arguments:
- node_state: bfloat16 [8192, 384], P(('rep', 'dom')), parts along dimension 0, may hold values from -6 to 6
- edge_state: bfloat16 [32768, 384], P(('rep', 'dom')), parts along dimension 0, may hold values from -6 to 6
- edge_source: int32 [32768], P(('rep', 'dom')), parts along dimension 0, may hold values from 0 to 383
- contact_block: int32 [128], P(('rep', 'dom')), parts along dimension 0, may hold values from 0 to 1
- contact_host: int32 [128, 1], P(('rep', 'dom')), parts along dimension 0, may hold values from 0 to 15; in each aligned block of 4 rows (0 to 3, 4 to 7, ...) at most 2 rows name the same one
- contact_remote: int32 [128], P(('rep', 'dom')), parts along dimension 0, may hold values from 0 to 1
- w_edge_in: bfloat16 [2304, 384], P('rep'), parts along dimension 0, may hold values from -0.1875 to 0.1875
- w_edge_out: bfloat16 [768, 384], P('rep'), parts along dimension 0, may hold values from -0.3125 to 0.3125
- w_node_in: bfloat16 [2304, 384], P('rep'), parts along dimension 0, may hold values from -0.1875 to 0.1875
- w_node_out: bfloat16 [768, 384], P('rep'), parts along dimension 0, may hold values from -0.3125 to 0.3125
- w_contact_in: bfloat16 [1536, 384], P('rep'), parts along dimension 0, may hold values from -0.21875 to 0.21875
- w_contact_out: bfloat16 [768, 384], P('rep'), parts along dimension 0, may hold values from -0.3125 to 0.3125
- node_cot: bfloat16 [8192, 384], P(('rep', 'dom')), parts along dimension 0, may hold values from -6 to 6
- edge_cot: bfloat16 [32768, 384], P(('rep', 'dom')), parts along dimension 0, may hold values from -6 to 6
Outputs:
- node_out: bfloat16 [8192, 384], P(('rep', 'dom')), parts along dimension 0
- edge_out: bfloat16 [32768, 384], P(('rep', 'dom')), parts along dimension 0
- node_grad: bfloat16 [8192, 384], P(('rep', 'dom')), parts along dimension 0
- edge_grad: bfloat16 [32768, 384], P(('rep', 'dom')), parts along dimension 0
- grad_edge_in: float32 [2304, 384], P('rep'), parts along dimension 0
- grad_edge_out: float32 [768, 384], P('rep'), parts along dimension 0
- grad_node_in: float32 [2304, 384], P('rep'), parts along dimension 0
- grad_node_out: float32 [768, 384], P('rep'), parts along dimension 0
- grad_contact_in: float32 [1536, 384], P('rep'), parts along dimension 0
- grad_contact_out: float32 [768, 384], P('rep'), parts along dimension 0
The draws below stay inside these ranges and needn't reach their ends.
There are 2 independent parts, one for each index of `rep`. The reference program is written for one: setup_inputs(seed, part) draws one part's arguments, and reference() takes and returns one part's arrays. A program takes and returns all parts, laid end to end along the dimension named above; each array names one. Nothing has to cross between parts.
Inputs may be any that keep to these rules, and one draw needn't show every extreme that they name: `contact_host`: the 4 rows of one partition name any one host partition at most 2 times, and 2 times in some partition.
All inputs are finite; a program needn't handle non-finite values.
Results may differ from the reference program's by a relative error of at most 0.0082.
Values may be sent and summed in bfloat16 or wider, within the bound.
No kernel may reach another device: no remote copies, remote signals or barrier semaphores. Data moves between devices by JAX's collectives and lax.ppermute only.
A program may use at most 128 MiB of HBM per device.

```python
import math
import jax
import jax.numpy as jnp
import numpy as np
from jax import lax

L = 384
BLOCK = 128
EPN = 4
RIM = 64
CAP = 2
NODE_DEV = 256
C_DEV = 4
NODES = 4096
EDGES = 16384
CONTACTS = 64
N_DOM = 16


def touch_ends(values, own_key, low, largest):
    dims = values.shape
    spot = [jax.random.randint(jax.random.fold_in(own_key, axis), (), 0, dims[axis]) for axis in range(len(dims))]
    values = values.at[tuple(spot)].set(low)
    longest = dims.index(max(dims))
    spot[longest] = (spot[longest] + 1) % dims[longest]
    return values.at[tuple(spot)].set(largest)


def block_scale(rng, shape, cuts, smallest, high):
    loudness, own = 1.0, jax.random.fold_in(rng, 6)
    for dim, parts in cuts:
        heights = jnp.exp(jax.random.uniform(jax.random.fold_in(own, dim), (parts,), jnp.float32, smallest / len(cuts), high / len(cuts)))
        loudness = loudness * jnp.repeat(heights, shape[dim] // parts).reshape([-1 if axis == dim else 1 for axis in range(len(shape))])
    return loudness


def deal_out(own_key, own, number, rows, amount, top, limit, skew):
    order = jax.random.permutation(own_key, amount)
    heavy_load, usual = portions_of(amount, rows * top, limit, skew, True), portions_of(amount, rows * top, limit, skew, False)
    places = jnp.arange(amount)

    def named(lengths, rotation):
        used = int((lengths > 0).sum())
        fixed = max(1, used // 4)
        passed = fixed + (places - fixed + rotation * (used - fixed)) % max(1, amount - fixed)
        return jnp.zeros((amount,), jnp.int32).at[order[jnp.where(places < fixed, places, passed)]].set(jnp.asarray(lengths, jnp.int32))

    lengths = jnp.where(number % 4 == 0, named(heavy_load, number // 4), named(usual, number - number // 4 - 1))
    mixed = jax.random.permutation(jax.random.fold_in(own, 3), amount)
    source_of, taker = mixed[0:amount // 2 * 2:2], mixed[1:amount // 2 * 2:2]
    margin = jnp.minimum(lengths[source_of] - 1, limit - lengths[taker]) // 2
    margin = jnp.where((source_of == order[0]) | (taker == order[0]) | (lengths[taker] == 0), 0, jnp.maximum(margin, 0))
    passed = jax.random.randint(jax.random.fold_in(own, 4), (amount // 2,), 0, 1 << 20) % (margin + 1)
    lengths = lengths.at[source_of].add(-passed).at[taker].add(passed)
    items = jnp.searchsorted(jnp.cumsum(lengths), jnp.arange(rows * top), side="right").astype(jnp.int32)
    grid = items.reshape(top, rows).T
    grid = grid[jax.random.permutation(jax.random.fold_in(own, 1), rows)]
    rotation = jax.random.randint(jax.random.fold_in(own, 2), (rows, 1), 0, top)
    return jnp.take_along_axis(grid, (jnp.arange(top)[None, :] + rotation) % top, axis=1)


def portions_of(number_of, total, most, slope, full):
    weights = [(1 << 20) // math.isqrt(standing ** slope) + 1 for standing in range(1, number_of + 1)]
    largest = most if full else min(most, max(-(-total // number_of), total * weights[0] // sum(weights)))
    least = 1 if total - largest >= number_of - 1 else 0
    holding, surplus = [largest] + [least] * (number_of - 1), total - largest - least * (number_of - 1)
    while surplus > 0:
        free = [i for i in range(1, number_of) if holding[i] < largest] or [i for i in range(1, number_of) if holding[i] < most]
        whole, left = sum([weights[i] for i in free]), surplus
        for i in free:
            more = min(most - holding[i], max(1, left * weights[i] // whole), surplus)
            holding[i] = holding[i] + more
            surplus = surplus - more
    return np.array(holding)


def gaussian(key, extent, scale, limit, pieces=(), kind=jnp.bfloat16):
    loudness = block_scale(key, extent, pieces, -0.22, 0.18) if pieces else 1.0
    array = jax.random.normal(key, extent, jnp.float32) * scale * loudness
    return jnp.minimum(jnp.maximum(array, -limit), limit).astype(kind)


def setup_inputs(seed: int = 0, part: int = 0) -> dict:
    keys = jax.random.split(jax.random.key(seed), 15)
    own_keys = jax.random.split(jax.random.fold_in(keys[14], part), 15)
    node_state = gaussian(own_keys[0], (NODES, L), 1.0, 6.0, ((0, 16),))
    edge_state = gaussian(own_keys[1], (EDGES, L), 1.0, 6.0, ((0, 16),))
    edge_source = touch_ends(jax.random.randint(own_keys[2], (EDGES,), 0, NODE_DEV + 2 * RIM), jax.random.fold_in(own_keys[2], 1), 0, (NODE_DEV + 2 * RIM) - 1).astype(jnp.int32)
    contact_block = touch_ends(jax.random.randint(own_keys[3], (CONTACTS,), 0, NODE_DEV // BLOCK), jax.random.fold_in(own_keys[3], 1), 0, (NODE_DEV // BLOCK) - 1).astype(jnp.int32)
    contact_host_keys = jax.random.split(jax.random.fold_in(own_keys[4], 1), CONTACTS // C_DEV)
    contact_host_turns = jax.random.permutation(jax.random.fold_in(own_keys[4], 3), CONTACTS // C_DEV)
    contact_host = jax.vmap(lambda own, number: deal_out(jax.random.fold_in(own_keys[4], 2), own, number, C_DEV, N_DOM, 1, CAP, 2))(contact_host_keys, contact_host_turns).reshape((CONTACTS, 1))
    contact_remote = touch_ends(jax.random.randint(own_keys[5], (CONTACTS,), 0, NODE_DEV // BLOCK), jax.random.fold_in(own_keys[5], 1), 0, (NODE_DEV // BLOCK) - 1).astype(jnp.int32)
    w_edge_in = gaussian(own_keys[6], (3 * L, L), (3 * L) ** -0.5, 0.1875)
    w_edge_out = gaussian(own_keys[7], (L, L), L ** -0.5, 0.3125)
    w_node_in = gaussian(own_keys[8], (3 * L, L), (3 * L) ** -0.5, 0.1875)
    w_node_out = gaussian(own_keys[9], (L, L), L ** -0.5, 0.3125)
    w_contact_in = gaussian(own_keys[10], (2 * L, L), (2 * L) ** -0.5, 0.21875)
    w_contact_out = gaussian(own_keys[11], (L, L), L ** -0.5, 0.3125)
    node_cot = gaussian(own_keys[12], (NODES, L), 1.0, 6.0, ((0, 16),))
    edge_cot = gaussian(own_keys[13], (EDGES, L), 1.0, 6.0, ((0, 16),))
    return dict(node_state=node_state, edge_state=edge_state, edge_source=edge_source, contact_block=contact_block, contact_host=contact_host, contact_remote=contact_remote, w_edge_in=w_edge_in, w_edge_out=w_edge_out, w_node_in=w_node_in, w_node_out=w_node_out, w_contact_in=w_contact_in, w_contact_out=w_contact_out, node_cot=node_cot, edge_cot=edge_cot)


norm_eps = 1e-05

def layer_norm(values):
    center = values - lax.optimization_barrier(jnp.mean(values, axis=-1, keepdims=True))
    scale = lax.rsqrt(lax.optimization_barrier(jnp.mean(center * center, axis=-1, keepdims=True)) + norm_eps)
    return center * scale

def layer_norm_back(values, upstream):
    center = values - lax.optimization_barrier(jnp.mean(values, axis=-1, keepdims=True))
    scale = lax.rsqrt(lax.optimization_barrier(jnp.mean(center * center, axis=-1, keepdims=True)) + norm_eps)
    normed = center * scale
    first = lax.optimization_barrier(jnp.mean(upstream, axis=-1, keepdims=True))
    second = lax.optimization_barrier(jnp.mean(upstream * normed, axis=-1, keepdims=True))
    return scale * (upstream - first - normed * second)

def forward_mlp(inputs, w_first, w_second):
    hidden_pre = jnp.dot(inputs, w_first, preferred_element_type=jnp.float32)
    hidden = jax.nn.silu(hidden_pre).astype(jnp.bfloat16)
    linear = jnp.dot(hidden, w_second, preferred_element_type=jnp.float32)
    return (hidden_pre, hidden, linear, layer_norm(linear))

def backward_mlp(inputs, hidden_pre, hidden, linear, w_second, upstream):
    d_linear = layer_norm_back(linear, upstream).astype(jnp.bfloat16)
    grad_second = jnp.dot(hidden.T, d_linear, preferred_element_type=jnp.float32)
    d_hidden = jnp.dot(d_linear, w_second.T, preferred_element_type=jnp.float32)
    sigma = jax.nn.sigmoid(hidden_pre)
    d_pre = (d_hidden * sigma * (1.0 + hidden_pre * (1.0 - sigma))).astype(jnp.bfloat16)
    grad_first = jnp.dot(inputs.T, d_pre, preferred_element_type=jnp.float32)
    return (d_pre, grad_first, grad_second)

def reference(node_state, edge_state, edge_source, contact_block, contact_host, contact_remote, w_edge_in, w_edge_out, w_node_in, w_node_out, w_contact_in, w_contact_out, node_cot, edge_cot):
    latent = node_state.shape[1]
    padded = jnp.pad(node_state, ((RIM, RIM), (0, 0)))
    edge_ids = jnp.arange(EDGES, dtype=jnp.int32)
    source_index = edge_ids // (EPN * NODE_DEV) * NODE_DEV + edge_source
    source_rows = padded[source_index]
    target_rows = jnp.repeat(node_state, EPN, axis=0)
    edge_input = jnp.concatenate([edge_state, source_rows, target_rows], axis=1)
    e_pre, e_hidden, e_linear, e_normed = forward_mlp(edge_input, w_edge_in, w_edge_out)
    edge_out = (edge_state.astype(jnp.float32) + e_normed).astype(jnp.bfloat16)
    mesh_sum = edge_out.astype(jnp.float32).reshape(NODES, EPN, latent).sum(axis=1).astype(jnp.bfloat16)
    offsets = jnp.arange(BLOCK, dtype=jnp.int32)
    receiver = jnp.arange(CONTACTS, dtype=jnp.int32) // C_DEV
    own_index = ((receiver * NODE_DEV + contact_block * BLOCK)[:, None] + offsets[None, :]).reshape(-1)
    remote_index = ((contact_host[:, 0] * NODE_DEV + contact_remote * BLOCK)[:, None] + offsets[None, :]).reshape(-1)
    contact_input = jnp.concatenate([node_state[own_index], node_state[remote_index]], axis=1)
    c_pre, c_hidden, c_linear, c_normed = forward_mlp(contact_input, w_contact_in, w_contact_out)
    message = c_normed.astype(jnp.bfloat16)
    contact_sum = jax.ops.segment_sum(message.astype(jnp.float32), own_index, NODES).astype(jnp.bfloat16)
    node_input = jnp.concatenate([node_state, mesh_sum, contact_sum], axis=1)
    n_pre, n_hidden, n_linear, n_normed = forward_mlp(node_input, w_node_in, w_node_out)
    node_out = (node_state.astype(jnp.float32) + n_normed).astype(jnp.bfloat16)
    d_node_pre, grad_node_in, grad_node_out = backward_mlp(node_input, n_pre, n_hidden, n_linear, w_node_out, node_cot.astype(jnp.float32))
    dx_node = jnp.dot(d_node_pre, w_node_in.T, preferred_element_type=jnp.float32)
    grad_h = node_cot.astype(jnp.float32) + dx_node[:, :latent]
    d_mesh = dx_node[:, latent:2 * latent].astype(jnp.bfloat16)
    d_contact = dx_node[:, 2 * latent:].astype(jnp.bfloat16)
    d_edge = edge_cot.astype(jnp.float32) + jnp.repeat(d_mesh.astype(jnp.float32), EPN, axis=0)
    d_edge_pre, grad_edge_in, grad_edge_out = backward_mlp(edge_input, e_pre, e_hidden, e_linear, w_edge_out, d_edge)
    dx_edge = jnp.dot(d_edge_pre, w_edge_in.T, preferred_element_type=jnp.float32)
    edge_grad = (d_edge + dx_edge[:, :latent]).astype(jnp.bfloat16)
    grad_h = grad_h + dx_edge[:, 2 * latent:].reshape(NODES, EPN, latent).sum(axis=1)
    spread = jax.ops.segment_sum(dx_edge[:, latent:2 * latent], source_index, NODES + 2 * RIM)
    grad_h = grad_h + spread[RIM:RIM + NODES]
    d_message = d_contact[own_index].astype(jnp.float32)
    d_contact_pre, grad_contact_in, grad_contact_out = backward_mlp(contact_input, c_pre, c_hidden, c_linear, w_contact_out, d_message)
    d_own = jnp.dot(d_contact_pre, w_contact_in[:latent].T, preferred_element_type=jnp.float32)
    d_remote = jnp.dot(d_contact_pre, w_contact_in[latent:].T, preferred_element_type=jnp.float32).astype(jnp.bfloat16)
    grad_h = grad_h + jax.ops.segment_sum(d_own, own_index, NODES)
    grad_h = grad_h + jax.ops.segment_sum(d_remote.astype(jnp.float32), remote_index, NODES)
    node_grad = grad_h.astype(jnp.bfloat16)
    return (node_out, edge_out, node_grad, edge_grad, grad_edge_in, grad_edge_out, grad_node_in, grad_node_out, grad_contact_in, grad_contact_out)
```

```python
import functools

import jax
import jax.numpy as jnp
from jax import lax
from jax.experimental import pallas as pl
from jax.experimental.pallas import tpu as pltpu
from jax.sharding import PartitionSpec as P

BLOCK = 128
EPN = 4
RIM = 64
EDGE_ROWS = 512
LABEL = 16
TILE = 32
STREAMS = 3
VMEM_LIMIT = 50 * 2**20
BF16 = jnp.bfloat16
F32 = jnp.float32


norm_eps = 1e-05


def exchange_orders(groups):
    bits = groups.bit_length() - 1
    low = list(range(bits - 1))
    turns = [r % max(1, len(low)) for r in range(STREAMS)]
    return [low[r:] + low[:r] + [bits - 1] for r in turns]


def return_orders(orders):
    heads = [(o[0], o[-2]) if s % 2 == 0 else (o[-2], o[0]) for s, o in enumerate(orders)]
    return [[*head, *o[1:-2], o[-1]] for head, o in zip(heads, orders)]


def places(order):
    bits = len(order)
    return [
        sum(((q >> (bits - 1 - i)) & 1) << b for i, b in enumerate(order)) for q in range(1 << bits)
    ]


def place_of(order, offset):
    bits = len(order)
    return sum(((offset >> b) & 1) << (bits - 1 - i) for i, b in enumerate(order))


def swap(value, bit):
    peers = lax.axis_size("dom")
    return lax.ppermute(value, "dom", [(i, i ^ (1 << bit)) for i in range(peers)])


def joined(values):
    return list(lax.optimization_barrier(tuple(values)))


def gather_step(held, orders, step):
    return [swap(value, order[-1 - step]) for value, order in zip(held, orders)]


def both(held, arrived):
    return [jnp.concatenate(pair, axis=0) for pair in zip(held, arrived)]


def added(halves, arrived):
    totals = [kept.astype(F32) + value.astype(F32) for (kept, _), value in zip(halves, arrived)]
    cut = totals[0].shape[0] // 2
    return [(total[:cut], total[cut:].astype(BF16)) for total in totals]


def dot(a, b):
    return jnp.dot(a, b, preferred_element_type=F32)


def dot_t(a, b):
    return lax.dot_general(a, b, (((1,), (1,)), ((), ())), preferred_element_type=F32)


def t_dot(a, b):
    return lax.dot_general(a, b, (((0,), (0,)), ((), ())), preferred_element_type=F32)


def sigmoid(z):
    return 0.5 * jnp.tanh(0.5 * z) + 0.5


def normed(values):
    center = values - jnp.mean(values, axis=-1, keepdims=True)
    scale = lax.rsqrt(jnp.mean(center * center, axis=-1, keepdims=True) + norm_eps)
    return center * scale, scale


def norm_back(values, upstream):
    unit, scale = normed(values)
    first = jnp.mean(upstream, axis=-1, keepdims=True)
    second = jnp.mean(upstream * unit, axis=-1, keepdims=True)
    return scale * (upstream - first - unit * second)


def tiles(rows):
    return [slice(i, i + TILE) for i in range(0, rows, TILE)]


def silu_tiles(z_ref, a_ref):
    for t in tiles(z_ref.shape[0]):
        z = z_ref[t]
        a_ref[t] = (z * sigmoid(z)).astype(BF16)


def silu_and_slope(z):
    s = sigmoid(z)
    a = z * s
    return a.astype(BF16), s + a * (1.0 - s)


def one_hot(condition):
    return jnp.where(condition, 1.0, 0.0).astype(BF16)


def iota(shape, axis):
    return lax.broadcasted_iota(jnp.int32, shape, axis)


def repeat_matrix(rows):
    shape = (rows, rows // EPN)
    return one_hot((iota(shape, 0) >> 2) == iota(shape, 1))


def sum_matrix(rows):
    shape = (rows // EPN, rows)
    return one_hot((iota(shape, 1) >> 2) == iota(shape, 0))


def parts_of(first, second, groups):
    shares = first // groups, second // groups
    if all(share % 8 == 0 and share * groups == size for share, size in zip(shares, (first, second))):
        return [(0, shares[0]), (first, shares[1])]
    return [(0, -(-(first + second) // (groups * 16)) * 16)]


def chunk_rows(parts):
    return -(-sum(rows for _, rows in parts) // 16) * 16


def total_rows(parts, groups):
    return max(base + rows * groups for base, rows in parts)


def starts_of(parts, device):
    return [pl.multiple_of(base + device * rows, 8) for base, rows in parts]


def deal(total_ref, kept_ref, sent_ref, order, parts, me):
    half, width = kept_ref.shape[0], kept_ref.shape[2]
    rows = kept_ref.shape[1] // STREAMS
    spare = rows - sum(count for _, count in parts)
    for q, offset in enumerate(places(order)):
        starts = starts_of(parts, me ^ offset)
        for s in range(STREAMS):
            columns = slice(s * width, (s + 1) * width)
            values = [
                total_ref[pl.ds(start, count), columns] for start, (_, count) in zip(starts, parts)
            ]
            if spare:
                values.append(jnp.zeros((spare, width), F32))
            value = jnp.concatenate(values, axis=0) if len(values) > 1 else values[0]
            if q < half:
                kept_ref[q, s * rows : (s + 1) * rows] = value.astype(kept_ref.dtype)
            else:
                sent_ref[q - half, s * rows : (s + 1) * rows] = value.astype(BF16)


def edge_forward(src_ref, before_ref, node_ref, after_ref, edge_ref, w_in_ref, w_out_ref,
                 out_ref, sum_ref, z_ref, y_ref, ext_ref, x_ref, a_ref):
    step = pl.program_id(0)
    count, latent = node_ref.shape
    rows = edge_ref.shape[0]
    targets = rows // EPN

    @pl.when(step == 0)
    def _():
        ext_ref[:RIM] = before_ref[...]
        ext_ref[RIM : RIM + count] = node_ref[...]
        ext_ref[RIM + count :] = after_ref[...]

    hit = one_hot(iota((count + 2 * RIM, rows), 0) == src_ref[0])
    own = node_ref[pl.ds(pl.multiple_of(step * targets, targets), targets), :]
    x_ref[:, :latent] = edge_ref[...]
    x_ref[:, latent : 2 * latent] = t_dot(hit, ext_ref[...]).astype(BF16)
    x_ref[:, 2 * latent :] = dot(repeat_matrix(rows), own).astype(BF16)
    z_ref[...] = dot(x_ref[...], w_in_ref[...])
    silu_tiles(z_ref, a_ref)
    y_ref[...] = dot(a_ref[...], w_out_ref[...])
    for t in tiles(rows):
        out_ref[t] = (edge_ref[t].astype(F32) + normed(y_ref[t])[0]).astype(BF16)
    sum_ref[...] = dot(sum_matrix(rows), out_ref[...]).astype(BF16)


def edge_backward(orders, parts, me_ref, src_ref, before_ref, node_ref, after_ref, edge_ref, z_ref, y_ref,
                  cot_ref, mesh_ref, partial_ref, w_in_ref, w_out_ref,
                  grad_ref, h_ref, low_ref, high_ref, kept_ref, sent_ref,
                  ext_ref, by_source_ref, by_target_ref, total_ref):
    step = pl.program_id(0)
    count, latent = node_ref.shape
    rows = edge_ref.shape[0]
    targets = rows // EPN

    @pl.when(step == 0)
    def _():
        by_source_ref[...] = jnp.zeros_like(by_source_ref)
        total_ref[...] = jnp.zeros_like(total_ref)

    upstream = cot_ref[...].astype(F32) + dot(repeat_matrix(rows), mesh_ref[...])
    d_y = norm_back(y_ref[...], upstream).astype(BF16)
    a, slope = silu_and_slope(z_ref[...])
    total_ref[3 * latent : 4 * latent] += t_dot(a, d_y)
    d_z = (dot_t(d_y, w_out_ref[...]) * slope).astype(BF16)
    total_ref[:latent] += t_dot(edge_ref[...], d_z)
    grad_ref[...] = (upstream + dot_t(d_z, w_in_ref[:latent])).astype(BF16)
    hit = one_hot(iota((count + 2 * RIM, rows), 0) == src_ref[0])
    by_source_ref[...] += dot(hit, d_z)
    place = pl.ds(pl.multiple_of(step * targets, targets), targets)
    by_target_ref[place, :] = dot(sum_matrix(rows), d_z)

    @pl.when(step == pl.num_programs(0) - 1)
    def _():
        ext_ref[:RIM] = before_ref[...]
        ext_ref[RIM : RIM + count] = node_ref[...]
        ext_ref[RIM + count :] = after_ref[...]
        by_source = by_source_ref[...].astype(BF16)
        total_ref[latent : 2 * latent] = t_dot(ext_ref[...], by_source)
        back = dot_t(by_source, w_in_ref[latent : 2 * latent])
        low_ref[...] = back[:RIM].astype(BF16)
        high_ref[...] = back[RIM + count :].astype(BF16)
        by_target = by_target_ref[...].astype(BF16)
        total_ref[2 * latent : 3 * latent] = t_dot(node_ref[...], by_target)
        h_ref[...] = (
            partial_ref[...] + back[RIM : RIM + count] + dot_t(by_target, w_in_ref[2 * latent :])
        )
        deal(total_ref, kept_ref, sent_ref, orders[0], parts, me_ref[0])


def node_and_contact(orders, node_parts, contact_parts, row_count, me_ref, host_ref, remote_ref, block_ref, *refs):
    count = 2 * STREAMS * row_count
    far = refs[:count]
    (node_ref, mesh_ref, cot_ref, nw_in_ref, nw_out_ref, cw_in_ref, cw_out_ref,
     out_ref, h_ref, d_mesh_ref, nkept_ref, nsent_ref, ckept_ref, csent_ref,
     *slab_refs) = refs[count : count + 16]
    (x_ref, z_ref, y_ref, sum_ref, total_ref, x_node_ref, d_contact_ref, g_ref,
     nw_in, nw_out, nkept, nsent, sems) = refs[count + 16 :]
    loads = [
        pltpu.make_async_copy(nw_in_ref, nw_in, sems.at[0]),
        pltpu.make_async_copy(nw_out_ref, nw_out, sems.at[1]),
    ]
    stores = [
        pltpu.make_async_copy(nkept, nkept_ref, sems.at[2]),
        pltpu.make_async_copy(nsent, nsent_ref, sems.at[3]),
    ]
    for copy in loads:
        copy.start()
    latent = node_ref.shape[1]
    width = latent // STREAMS
    me = me_ref[0]
    chunk = min(4, row_count)
    blocks = node_ref.shape[0] // BLOCK
    half = nkept_ref.shape[0]

    def own_rows(row):
        return pl.ds(pl.multiple_of(block_ref[row] * BLOCK, BLOCK), BLOCK)

    sum_ref[...] = jnp.zeros_like(sum_ref)
    for row in range(row_count):
        rows = slice(row * BLOCK, (row + 1) * BLOCK)
        x_ref[rows, :latent] = node_ref[own_rows(row), :]
        for s, order in enumerate(orders):
            columns = slice(latent + s * width, latent + (s + 1) * width)
            near, away = far[2 * (row * STREAMS + s)], far[2 * (row * STREAMS + s) + 1]
            is_near = place_of(order, host_ref[row] ^ me) < half

            @pl.when(is_near)
            def _():
                x_ref[rows, columns] = near[0]

            @pl.when(jnp.logical_not(is_near))
            def _():
                x_ref[rows, columns] = away[0]
    for first in range(0, row_count, chunk):
        rows = slice(first * BLOCK, (first + chunk) * BLOCK)
        z = dot(x_ref[rows], cw_in_ref[...])
        y = dot(silu_and_slope(z)[0], cw_out_ref[...])
        z_ref[rows] = z
        y_ref[rows] = y
        message = normed(y)[0].astype(BF16).astype(F32)
        for row in range(first, first + chunk):
            part = message[(row - first) * BLOCK : (row - first + 1) * BLOCK]
            sum_ref[own_rows(row), :] += part

    for copy in loads:
        copy.wait()
    node = node_ref[...]
    x_node_ref[:, :latent] = node
    x_node_ref[:, latent : 2 * latent] = mesh_ref[...]
    x_node_ref[:, 2 * latent :] = sum_ref[...].astype(BF16)
    z = dot(x_node_ref[...], nw_in[...])
    a, slope = silu_and_slope(z)
    y = dot(a, nw_out[...])
    out_ref[...] = (node.astype(F32) + normed(y)[0]).astype(BF16)
    upstream = cot_ref[...].astype(F32)
    d_y = norm_back(y, upstream).astype(BF16)
    total_ref[3 * latent : 4 * latent] = t_dot(a, d_y)
    d_z = (dot_t(d_y, nw_out[...]) * slope).astype(BF16)
    total_ref[: 3 * latent] = t_dot(x_node_ref[...], d_z)
    if total_ref.shape[0] > 4 * latent:
        total_ref[4 * latent :] = jnp.zeros((total_ref.shape[0] - 4 * latent, latent), F32)
    d_x = dot_t(d_z, nw_in[...])
    h_ref[...] = upstream + d_x[:, :latent]
    d_mesh_ref[...] = d_x[:, latent : 2 * latent].astype(BF16)
    d_contact_ref[...] = d_x[:, 2 * latent :].astype(BF16).astype(F32)
    deal(total_ref, nkept, nsent, orders[1], node_parts, me)
    for copy in stores:
        copy.start()

    total_ref[: 3 * latent] = jnp.zeros((3 * latent, latent), F32)
    if total_ref.shape[0] > 3 * latent:
        total_ref[3 * latent :] = jnp.zeros((total_ref.shape[0] - 3 * latent, latent), F32)
    for first in range(0, row_count, chunk):
        rows = slice(first * BLOCK, (first + chunk) * BLOCK)
        for row in range(first, first + chunk):
            part = slice((row - first) * BLOCK, (row - first + 1) * BLOCK)
            g_ref[part, :latent] = d_contact_ref[own_rows(row), :]
        d_y = norm_back(y_ref[rows], g_ref[:, :latent]).astype(BF16)
        a, slope = silu_and_slope(z_ref[rows])
        total_ref[2 * latent : 3 * latent] += t_dot(a, d_y)
        d_z = (dot_t(d_y, cw_out_ref[...]) * slope).astype(BF16)
        total_ref[: 2 * latent] += t_dot(x_ref[rows], d_z)
        g_ref[...] = dot_t(d_z, cw_in_ref[...])
        for row in range(first, first + chunk):
            part = slice((row - first) * BLOCK, (row - first + 1) * BLOCK)
            h_ref[own_rows(row), :] += g_ref[part, :latent]
            label = (host_ref[row] * blocks + remote_ref[row]).astype(F32)
            cut = latent
            for ref in slab_refs:
                columns = ref.shape[2]
                ref[row, :BLOCK] = g_ref[part, cut : cut + columns].astype(BF16)
                ref[row, BLOCK:] = jnp.full((LABEL, columns), label, F32).astype(BF16)
                cut += columns
    deal(total_ref, ckept_ref, csent_ref, orders[2], contact_parts, me)
    for copy in stores:
        copy.wait()


def pick_blocks(orders, blocks, row_count, me_ref, *refs):
    named, slabs, outs, sems = refs[:3], refs[3:6], refs[6:9], refs[9]
    copies = []
    for s, order in enumerate(orders):
        for i in range(row_count):
            spot = place_of(order, named[s][i] ^ me_ref[0])
            spot = jnp.where(spot < slabs[s].shape[0] // blocks, spot, 0)
            block = spot * blocks + named[s][row_count + i]
            copies.append(
                pltpu.make_async_copy(slabs[s].at[block], outs[s].at[i], sems.at[len(copies)])
            )
            copies[-1].start()
    for copy in copies:
        copy.wait()


def add_to_places(orders, blocks, half, me_ref, host_ref, remote_ref, *refs):
    own, arrived, outs = refs[:2], refs[2:4], refs[4:]
    row_count = own[0].shape[0]
    width = outs[0].shape[2]
    views = [(0, slice(0, width)), (0, slice(width, 2 * width)), (1, slice(0, width))]
    me = me_ref[0]
    for s, order in enumerate(orders):
        bits = len(order)
        out = outs[s]
        slots = out.shape[0]
        first = half * slots
        array, columns = views[s]
        marks = [arrived[array][i, BLOCK:, columns].astype(F32)[:1] for i in range(row_count)]

        def step(slot, carry):
            place = (first + slot) // blocks
            offset = sum(((place >> (bits - 1 - i)) & 1) << b for i, b in enumerate(order))
            label = ((me ^ offset) * blocks + slot % blocks).astype(F32)
            value = jnp.zeros((BLOCK, out.shape[2]), F32)
            for i, mark in enumerate(marks):
                hit = jnp.where(mark == label, 1.0, 0.0)
                value = value + arrived[array][i, :BLOCK, columns].astype(F32) * hit
            out[slot] = value.astype(out.dtype)
            return carry

        lax.fori_loop(0, slots, step, 0)
        for i in range(row_count):
            spot = place_of(order, host_ref[i] ^ me) * blocks + remote_ref[i] - first

            @pl.when(jnp.logical_and(spot >= 0, spot < slots))
            def _():
                total = out[spot].astype(F32) + own[array][i, :BLOCK, columns].astype(F32)
                out[spot] = total.astype(out.dtype)


def unpack(orders, parts, half_index, me_ref, *refs):
    halves, rest = refs[:STREAMS], refs[STREAMS:]
    outs, rows_refs, sems = rest[-3 * STREAMS - 1 : -STREAMS - 1], rest[-STREAMS - 1 : -1], rest[-1]
    copies = []
    for s, order in enumerate(orders):
        count, width = halves[s].shape[0], halves[s].shape[2]
        rows = halves[s].shape[1] // STREAMS
        for q in range(count):
            for c in range(STREAMS):
                value = halves[s][q, c * rows : (c + 1) * rows].astype(F32)
                rows_refs[s][q, :, c * width : (c + 1) * width] = value
            device = me_ref[0] ^ places(order)[half_index * count + q]
            done = 0
            for p, (_, share) in enumerate(parts[s]):
                start = pl.multiple_of(device * share, 8)
                copy = pltpu.make_async_copy(
                    rows_refs[s].at[q, pl.ds(done, share)],
                    outs[2 * s + p].at[pl.ds(start, share)],
                    sems.at[len(copies)],
                )
                copy.start()
                copies.append(copy)
                done += share
    for copy in copies:
        copy.wait()


def unpack_whole(order, me_ref, near_ref, far_ref, first_ref, second_ref, total_ref):
    half, width = near_ref.shape[0], near_ref.shape[2]
    rows = near_ref.shape[1] // STREAMS
    for q, offset in enumerate(places(order)):
        ref, place = (near_ref, q) if q < half else (far_ref, q - half)
        start = pl.multiple_of((me_ref[0] ^ offset) * rows, 8)
        for s in range(STREAMS):
            value = ref[place, s * rows : (s + 1) * rows].astype(F32)
            total_ref[pl.ds(start, rows), s * width : (s + 1) * width] = value
    cut = first_ref.shape[0]
    first_ref[...] = total_ref[:cut]
    second_ref[...] = total_ref[cut : cut + second_ref.shape[0]]


def params(axes=0):
    return pltpu.CompilerParams(
        vmem_limit_bytes=VMEM_LIMIT,
        dimension_semantics=("arbitrary",) * axes if axes else None,
    )


def cost(flops, moved):
    return pl.CostEstimate(flops=flops, bytes_accessed=moved, transcendentals=0)


def whole(array_shape):
    return pl.BlockSpec(array_shape, lambda *_: (0,) * len(array_shape))


def struct(shape, dtype):
    return jax.ShapeDtypeStruct(shape, dtype)


def on_device(
    node_state,
    edge_state,
    edge_source,
    contact_block,
    contact_host,
    contact_remote,
    w_edge_in,
    w_edge_out,
    w_node_in,
    w_node_out,
    w_contact_in,
    w_contact_out,
    node_cot,
    edge_cot,
):
    node_count, latent = node_state.shape
    edge_count = edge_state.shape[0]
    groups = lax.axis_size("dom")
    blocks = node_count // BLOCK
    row_count = contact_block.shape[0]
    width = latent // STREAMS
    orders = exchange_orders(groups)
    me = lax.axis_index("dom").astype(jnp.int32).reshape(1)
    host = contact_host[:, 0]
    smem = pl.BlockSpec(memory_space=pltpu.SMEM)
    anywhere = pl.BlockSpec(memory_space=pl.ANY)

    up = [(i, i + 1) for i in range(groups - 1)]
    down = [(j, i) for i, j in up]
    before = lax.ppermute(node_state[node_count - RIM :], "dom", up)
    after = lax.ppermute(node_state[:RIM], "dom", down)
    last = len(orders[0]) - 1
    far_bit = orders[0][-1]
    half = groups // 2
    rows_named = jnp.concatenate([host, contact_remote])
    arrived, before, after, *named = joined(
        [swap(node_state, far_bit), before, after]
        + [swap(rows_named, order[0]) for order in orders]
    )
    pair = jnp.stack([node_state, arrived])
    slabs = [pair[:, :, s * width : (s + 1) * width] for s in range(STREAMS)]
    for step in range(1, last):
        if step == last - 1:
            *slabs, before = joined([*slabs, before])
        arrived = gather_step(slabs, orders, step)
        if step < last - 1:
            slabs = both(slabs, joined(arrived))

    steps = edge_count // EDGE_ROWS
    sources = edge_source.reshape(steps, 1, EDGE_ROWS)
    edge_block = pl.BlockSpec((EDGE_ROWS, latent), lambda i: (i, 0))
    node_block = pl.BlockSpec((EDGE_ROWS // EPN, latent), lambda i: (i, 0))
    source_block = pl.BlockSpec((1, 1, EDGE_ROWS), lambda i: (i, 0, 0))
    rim_block = whole((RIM, latent))
    extended_rows = node_count + 2 * RIM
    edge_out, mesh_sum, e_pre, e_linear = pl.pallas_call(
        edge_forward,
        grid=(steps,),
        in_specs=[
            source_block,
            rim_block,
            whole(node_state.shape),
            rim_block,
            edge_block,
            whole(w_edge_in.shape),
            whole(w_edge_out.shape),
        ],
        out_specs=[edge_block, node_block, edge_block, edge_block],
        out_shape=[
            struct((edge_count, latent), BF16),
            struct((node_count, latent), BF16),
            struct((edge_count, latent), F32),
            struct((edge_count, latent), F32),
        ],
        scratch_shapes=[
            pltpu.VMEM((extended_rows, latent), BF16),
            pltpu.VMEM((EDGE_ROWS, 3 * latent), BF16),
            pltpu.VMEM((EDGE_ROWS, latent), BF16),
        ],
        compiler_params=params(1),
        cost_estimate=cost(2 * edge_count * latent * latent * 6, edge_count * latent * 16),
        name="edge_forward",
    )(sources, before, node_state, after, edge_state, w_edge_in, w_edge_out)

    *arrived, mesh_sum = joined([*arrived, mesh_sum])
    slabs = [
        slab.reshape(half * blocks, BLOCK, width) for slab in both(slabs, arrived)
    ]
    picked = pl.pallas_call(
        functools.partial(pick_blocks, orders, blocks, row_count),
        in_specs=[smem] * (1 + STREAMS) + [anywhere] * STREAMS,
        out_specs=[anywhere] * STREAMS,
        out_shape=[struct((row_count, BLOCK, width), BF16)] * STREAMS,
        scratch_shapes=[pltpu.SemaphoreType.DMA((STREAMS * row_count,))],
        compiler_params=params(),
        cost_estimate=cost(0, 2**20),
        name="pick_blocks",
    )(me, *named, *slabs)
    answered = [swap(value, order[0]) for value, order in zip(picked, orders)]

    def near_spec(row, s):
        def index(i, me_ref, host_ref, remote_ref, block_ref):
            spot = place_of(orders[s], host_ref[row] ^ me_ref[0])
            return (jnp.where(spot < half, spot * blocks + remote_ref[row], 0), 0, 0)

        return pl.BlockSpec((1, BLOCK, width), index)

    def answer_spec(row):
        return pl.BlockSpec((1, BLOCK, width), lambda *_: (row, 0, 0))

    far = []
    for row in range(row_count):
        for s in range(STREAMS):
            far += [(near_spec(row, s), slabs[s]), (answer_spec(row), answered[s])]
    far_specs, far_args = [spec for spec, _ in far], [arg for _, arg in far]
    matrices = [(w_edge_in, w_edge_out), (w_node_in, w_node_out), (w_contact_in, w_contact_out)]
    parts = [parts_of(first.shape[0], second.shape[0], groups) for first, second in matrices]
    pair_rows = [chunk_rows(part) for part in parts]
    halves = lambda rows: [struct((half, rows * STREAMS, width), BF16)] * 2
    labelled = [
        struct((row_count, BLOCK + LABEL, columns), BF16) for columns in (2 * width, latent - 2 * width)
    ]
    b_out = [
        struct((node_count, latent), BF16),
        struct((node_count, latent), F32),
        struct((node_count, latent), BF16),
        *halves(pair_rows[1]),
        *halves(pair_rows[2]),
        *labelled,
    ]
    b_args = [node_state, mesh_sum, node_cot, w_node_in, w_node_out, w_contact_in, w_contact_out]
    contact_rows = row_count * BLOCK
    chunk_length = min(4, row_count) * BLOCK
    (node_out, partial_h, d_mesh, n_kept, n_sent, c_kept, c_sent, *away) = pl.pallas_call(
        functools.partial(node_and_contact, orders, parts[1], parts[2], row_count),
        grid_spec=pltpu.PrefetchScalarGridSpec(
            num_scalar_prefetch=4,
            grid=(1,),
            in_specs=far_specs
            + [anywhere if 3 <= i <= 4 else whole(arg.shape) for i, arg in enumerate(b_args)],
            out_specs=[
                anywhere if 3 <= i <= 4 else whole(out.shape) for i, out in enumerate(b_out)
            ],
            scratch_shapes=[
                pltpu.VMEM((contact_rows, 2 * latent), BF16),
                pltpu.VMEM((contact_rows, latent), F32),
                pltpu.VMEM((contact_rows, latent), F32),
                pltpu.VMEM((node_count, latent), F32),
                pltpu.VMEM((max(total_rows(part, groups) for part in parts[1:]), latent), F32),
                pltpu.VMEM((node_count, 3 * latent), BF16),
                pltpu.VMEM((node_count, latent), F32),
                pltpu.VMEM((chunk_length, 2 * latent), F32),
                pltpu.VMEM(w_node_in.shape, BF16),
                pltpu.VMEM(w_node_out.shape, BF16),
                pltpu.VMEM(b_out[3].shape, BF16),
                pltpu.VMEM(b_out[4].shape, BF16),
                pltpu.SemaphoreType.DMA((4,)),
            ],
        ),
        out_shape=b_out,
        compiler_params=params(1),
        cost_estimate=cost(2 * (contact_rows * 9 + node_count * 12) * latent * latent, 12 * 2**20),
        name="node_and_contact",
    )(me, host, contact_remote, contact_block, *far_args, *b_args)

    back = return_orders(orders)
    away_arrived = [swap(value, order[0]) for value, order in zip(away, back[1:])]
    n_arrived, c_arrived = swap(n_sent, orders[1][0]), swap(c_sent, orders[2][0])

    edge_grad, near_h, low, high, e_kept, e_sent = pl.pallas_call(
        functools.partial(edge_backward, orders, parts[0]),
        grid=(steps,),
        in_specs=[
            smem,
            source_block,
            rim_block,
            whole(node_state.shape),
            rim_block,
            edge_block,
            edge_block,
            edge_block,
            edge_block,
            node_block,
            whole((node_count, latent)),
            whole(w_edge_in.shape),
            whole(w_edge_out.shape),
        ],
        out_specs=[
            edge_block,
            whole((node_count, latent)),
            rim_block,
            rim_block,
            *[whole((half, pair_rows[0] * STREAMS, width))] * 2,
        ],
        out_shape=[
            struct((edge_count, latent), BF16),
            struct((node_count, latent), F32),
            struct((RIM, latent), BF16),
            struct((RIM, latent), BF16),
            *halves(pair_rows[0]),
        ],
        scratch_shapes=[
            pltpu.VMEM((extended_rows, latent), BF16),
            pltpu.VMEM((extended_rows, latent), F32),
            pltpu.VMEM((node_count, latent), F32),
            pltpu.VMEM((total_rows(parts[0], groups), latent), F32),
        ],
        compiler_params=params(1),
        cost_estimate=cost(2 * edge_count * latent * latent * 8, edge_count * latent * 20),
        name="edge_backward",
    )(me, sources, before, node_state, after, edge_state, e_pre, e_linear, edge_cot, d_mesh,
      partial_h, w_edge_in, w_edge_out)

    *away_arrived, e_sent = joined([*away_arrived, e_sent])
    e_arrived = swap(e_sent, orders[0][0])
    slots = half * blocks // 2
    def places_call(half_index, dtype, own, arrived):
        return pl.pallas_call(
            functools.partial(add_to_places, back, blocks, half_index),
            in_specs=[smem] * 3 + [pl.BlockSpec(memory_space=pltpu.VMEM)] * 4,
            out_specs=[pl.BlockSpec(memory_space=pltpu.VMEM)] * STREAMS,
            out_shape=[struct((slots, BLOCK, width), dtype)] * STREAMS,
            compiler_params=params(),
            cost_estimate=cost(0, 3 * 2**20),
            name="add_to_places",
        )(me, host, contact_remote, *own, *arrived)

    away_sent = places_call(1, BF16, away, away_arrived)
    n_arrived, c_arrived, *away_sent = joined([n_arrived, c_arrived, *away_sent])
    arrived = [swap(sent, order[1]) for sent, order in zip(away_sent, back)]
    arrived[0], *blocks_in = joined([arrived[0], *away, *away_arrived])
    away_kept = places_call(0, F32, blocks_in[:2], blocks_in[2:])
    *arrived, e_arrived = joined([*arrived, e_arrived])
    away = list(zip(away_kept, away_sent))
    away = added(away, arrived)
    weights = added(
        [(e_kept, e_sent), (n_kept, n_sent), (c_kept, c_sent)], [e_arrived, n_arrived, c_arrived]
    )
    for step in range(1, last - 1):
        sent = [jnp.concatenate([a[1], w[1]], axis=1) for a, w in zip(away, weights)]
        arrived = joined([swap(value, order[step]) for value, order in zip(sent, orders)])
        away = added(away, [value[:, :BLOCK] for value in arrived])
        weights = added(weights, [value[:, BLOCK:] for value in arrived])
    arrived = joined([swap(w[1], order[last - 1]) for w, order in zip(weights, orders)])
    mine = jnp.concatenate(
        [(w[0] + value.astype(F32)).astype(BF16) for w, value in zip(weights, arrived)], axis=1
    )
    mine, low, high = joined([mine, low, high])
    theirs, low, high = joined(
        [swap(mine, far_bit), lax.ppermute(low, "dom", down), lax.ppermute(high, "dom", up)]
    )
    pair = (mine.astype(F32) + theirs[::-1].astype(F32)).astype(BF16)
    away_sent = jnp.concatenate([sent for _, sent in away], axis=2)
    pair, away_sent = joined([pair, away_sent])
    returned = swap(away_sent, far_bit)
    cuts = [sum(pair_rows[:s]) * STREAMS for s in range(STREAMS + 1)]
    sums = [pair[:, cuts[s] : cuts[s + 1]] for s in range(STREAMS)]
    for step in range(1, last):
        sums = both(sums, joined(gather_step(sums, orders, step)))
    gathered = list(zip(sums, gather_step(sums, orders, last)))
    kept = jnp.concatenate([kept for kept, _ in away], axis=2)
    returned = (kept + returned.astype(F32)).reshape(node_count, latent)
    vmem = pl.BlockSpec(memory_space=pltpu.VMEM)
    if all(len(part) == 2 for part in parts):
        summed = []
        for side in range(2):
            summed = pl.pallas_call(
                functools.partial(unpack, orders, parts, side),
                in_specs=[smem] + [vmem] * STREAMS + [anywhere] * len(summed),
                out_specs=[anywhere] * (2 * STREAMS),
                out_shape=[struct(w.shape, F32) for pair in matrices for w in pair],
                scratch_shapes=[
                    *[pltpu.VMEM((half, rows, latent), F32) for rows in pair_rows],
                    pltpu.SemaphoreType.DMA((2 * STREAMS * half,)),
                ],
                input_output_aliases={1 + STREAMS + i: i for i in range(len(summed))},
                compiler_params=params(),
                cost_estimate=cost(0, half * sum(pair_rows) * latent * 10),
                name="unpack",
            )(me, *[pair[side] for pair in gathered], *summed)
    else:
        summed = []
        for s, (first, second) in enumerate(matrices):
            summed += pl.pallas_call(
                functools.partial(unpack_whole, orders[s]),
                in_specs=[smem] + [vmem] * 2,
                out_specs=[vmem] * 2,
                out_shape=[struct(first.shape, F32), struct(second.shape, F32)],
                scratch_shapes=[pltpu.VMEM((pair_rows[s] * groups, latent), F32)],
                compiler_params=params(),
                name="unpack_whole",
            )(me, *gathered[s])

    rims = jnp.concatenate(
        [
            high.astype(F32),
            jnp.zeros((node_count - 2 * RIM, latent), F32),
            low.astype(F32),
        ],
        axis=0,
    )
    node_grad = (near_h + rims + returned).astype(BF16)
    return (node_out, edge_out, node_grad, edge_grad, *summed)


def solution(mesh):
    rows = P(("rep", "dom"), None)
    flat = P(("rep", "dom"))
    weight = P("rep", None)
    in_specs = (rows, rows, flat, flat, rows, flat) + (weight,) * 6 + (rows, rows)
    out_specs = (rows,) * 4 + (weight,) * 6
    return jax.shard_map(
        on_device, mesh=mesh, in_specs=in_specs, out_specs=out_specs, check_vma=False
    )
```

```python
import functools

import jax
import jax.numpy as jnp
from jax import lax
from jax.experimental import pallas as pl
from jax.experimental.pallas import tpu as pltpu
from jax.sharding import PartitionSpec as P

BLOCK = 128
EPN = 4
RIM = 64
EDGE_ROWS = 512
LABEL = 16
TILE = 32
STREAMS = 3
VMEM_LIMIT = 50 * 2**20
BF16 = jnp.bfloat16
F32 = jnp.float32


norm_eps = 1e-05


def exchange_orders(groups):
    bits = groups.bit_length() - 1
    low = list(range(bits - 1))
    turns = [r % max(1, len(low)) for r in range(STREAMS)]
    return [low[r:] + low[:r] + [bits - 1] for r in turns]


def return_orders(orders):
    heads = [(o[0], o[-2]) if s % 2 == 0 else (o[-2], o[0]) for s, o in enumerate(orders)]
    return [[*head, *o[1:-2], o[-1]] for head, o in zip(heads, orders)]


def places(order):
    bits = len(order)
    return [
        sum(((q >> (bits - 1 - i)) & 1) << b for i, b in enumerate(order)) for q in range(1 << bits)
    ]


def place_of(order, offset):
    bits = len(order)
    return sum(((offset >> b) & 1) << (bits - 1 - i) for i, b in enumerate(order))


def swap(value, bit):
    peers = lax.axis_size("dom")
    return lax.ppermute(value, "dom", [(i, i ^ (1 << bit)) for i in range(peers)])


def swap_rims(first, last):
    peers = lax.axis_size("dom")
    odd = lax.axis_index("dom") % 2 == 1
    pairs = [[(i, i + 1) for i in range(start, peers - 1, 2)] for start in range(2)]
    both_ways = [pair + [(j, i) for i, j in pair] for pair in pairs]
    inner = lax.ppermute(jnp.where(odd, first, last), "dom", both_ways[0])
    outer = lax.ppermute(jnp.where(odd, last, first), "dom", both_ways[1])
    return inner, outer


def sorted_rims(inner, outer):
    odd = lax.axis_index("dom") % 2 == 1
    return jnp.where(odd, inner, outer), jnp.where(odd, outer, inner)


def joined(values):
    return list(lax.optimization_barrier(tuple(values)))


def gather_step(held, orders, step):
    return [swap(value, order[-1 - step]) for value, order in zip(held, orders)]


def both(held, arrived):
    return [jnp.concatenate(pair, axis=0) for pair in zip(held, arrived)]


def added(halves, arrived):
    totals = [kept.astype(F32) + value.astype(F32) for (kept, _), value in zip(halves, arrived)]
    cut = totals[0].shape[0] // 2
    return [(total[:cut], total[cut:].astype(BF16)) for total in totals]


def dot(a, b):
    return jnp.dot(a, b, preferred_element_type=F32)


def dot_t(a, b):
    return lax.dot_general(a, b, (((1,), (1,)), ((), ())), preferred_element_type=F32)


def t_dot(a, b):
    return lax.dot_general(a, b, (((0,), (0,)), ((), ())), preferred_element_type=F32)


def sigmoid(z):
    return 0.5 * jnp.tanh(0.5 * z) + 0.5


def normed(values):
    center = values - jnp.mean(values, axis=-1, keepdims=True)
    scale = lax.rsqrt(jnp.mean(center * center, axis=-1, keepdims=True) + norm_eps)
    return center * scale, scale


def norm_back(values, upstream):
    unit, scale = normed(values)
    first = jnp.mean(upstream, axis=-1, keepdims=True)
    second = jnp.mean(upstream * unit, axis=-1, keepdims=True)
    return scale * (upstream - first - unit * second)


def tiles(rows):
    return [slice(i, i + TILE) for i in range(0, rows, TILE)]


def silu_tiles(z_ref, a_ref):
    for t in tiles(z_ref.shape[0]):
        z = z_ref[t]
        a_ref[t] = (z * sigmoid(z)).astype(BF16)


def silu_and_slope(z):
    s = sigmoid(z)
    a = z * s
    return a.astype(BF16), s + a * (1.0 - s)


def one_hot(condition):
    return jnp.where(condition, 1.0, 0.0).astype(BF16)


def iota(shape, axis):
    return lax.broadcasted_iota(jnp.int32, shape, axis)


def repeat_matrix(rows):
    shape = (rows, rows // EPN)
    return one_hot((iota(shape, 0) >> 2) == iota(shape, 1))


def sum_matrix(rows):
    shape = (rows // EPN, rows)
    return one_hot((iota(shape, 1) >> 2) == iota(shape, 0))


def parts_of(first, second, groups):
    shares = first // groups, second // groups
    if all(share % 8 == 0 and share * groups == size for share, size in zip(shares, (first, second))):
        return [(0, shares[0]), (first, shares[1])]
    return [(0, -(-(first + second) // (groups * 16)) * 16)]


def chunk_rows(parts):
    return -(-sum(rows for _, rows in parts) // 16) * 16


def total_rows(parts, groups):
    return max(base + rows * groups for base, rows in parts)


def starts_of(parts, device):
    return [pl.multiple_of(base + device * rows, 8) for base, rows in parts]


def deal(total_ref, kept_ref, sent_ref, order, parts, me):
    half, width = kept_ref.shape[0], kept_ref.shape[2]
    rows = kept_ref.shape[1] // STREAMS
    spare = rows - sum(count for _, count in parts)
    for q, offset in enumerate(places(order)):
        starts = starts_of(parts, me ^ offset)
        for s in range(STREAMS):
            columns = slice(s * width, (s + 1) * width)
            values = [
                total_ref[pl.ds(start, count), columns] for start, (_, count) in zip(starts, parts)
            ]
            if spare:
                values.append(jnp.zeros((spare, width), F32))
            value = jnp.concatenate(values, axis=0) if len(values) > 1 else values[0]
            if q < half:
                kept_ref[q, s * rows : (s + 1) * rows] = value.astype(kept_ref.dtype)
            else:
                sent_ref[q - half, s * rows : (s + 1) * rows] = value.astype(BF16)


def edge_forward(src_ref, before_ref, node_ref, after_ref, edge_ref, w_in_ref, w_out_ref,
                 out_ref, sum_ref, z_ref, y_ref, ext_ref, x_ref, a_ref):
    step = pl.program_id(0)
    count, latent = node_ref.shape
    rows = edge_ref.shape[0]
    targets = rows // EPN

    @pl.when(step == 0)
    def _():
        ext_ref[:RIM] = before_ref[...]
        ext_ref[RIM : RIM + count] = node_ref[...]
        ext_ref[RIM + count :] = after_ref[...]

    hit = one_hot(iota((count + 2 * RIM, rows), 0) == src_ref[0])
    own = node_ref[pl.ds(pl.multiple_of(step * targets, targets), targets), :]
    x_ref[:, :latent] = edge_ref[...]
    x_ref[:, latent : 2 * latent] = t_dot(hit, ext_ref[...]).astype(BF16)
    x_ref[:, 2 * latent :] = dot(repeat_matrix(rows), own).astype(BF16)
    z_ref[...] = dot(x_ref[...], w_in_ref[...])
    silu_tiles(z_ref, a_ref)
    y_ref[...] = dot(a_ref[...], w_out_ref[...])
    for t in tiles(rows):
        out_ref[t] = (edge_ref[t].astype(F32) + normed(y_ref[t])[0]).astype(BF16)
    sum_ref[...] = dot(sum_matrix(rows), out_ref[...]).astype(BF16)


def edge_backward(orders, parts, me_ref, src_ref, before_ref, node_ref, after_ref, edge_ref, z_ref, y_ref,
                  cot_ref, mesh_ref, partial_ref, w_in_ref, w_out_ref,
                  grad_ref, h_ref, low_ref, high_ref, kept_ref, sent_ref,
                  ext_ref, by_source_ref, by_target_ref, total_ref):
    step = pl.program_id(0)
    count, latent = node_ref.shape
    rows = edge_ref.shape[0]
    targets = rows // EPN

    @pl.when(step == 0)
    def _():
        by_source_ref[...] = jnp.zeros_like(by_source_ref)
        total_ref[...] = jnp.zeros_like(total_ref)

    upstream = cot_ref[...].astype(F32) + dot(repeat_matrix(rows), mesh_ref[...])
    d_y = norm_back(y_ref[...], upstream).astype(BF16)
    a, slope = silu_and_slope(z_ref[...])
    total_ref[3 * latent : 4 * latent] += t_dot(a, d_y)
    d_z = (dot_t(d_y, w_out_ref[...]) * slope).astype(BF16)
    total_ref[:latent] += t_dot(edge_ref[...], d_z)
    grad_ref[...] = (upstream + dot_t(d_z, w_in_ref[:latent])).astype(BF16)
    hit = one_hot(iota((count + 2 * RIM, rows), 0) == src_ref[0])
    by_source_ref[...] += dot(hit, d_z)
    place = pl.ds(pl.multiple_of(step * targets, targets), targets)
    by_target_ref[place, :] = dot(sum_matrix(rows), d_z)

    @pl.when(step == pl.num_programs(0) - 1)
    def _():
        ext_ref[:RIM] = before_ref[...]
        ext_ref[RIM : RIM + count] = node_ref[...]
        ext_ref[RIM + count :] = after_ref[...]
        by_source = by_source_ref[...].astype(BF16)
        total_ref[latent : 2 * latent] = t_dot(ext_ref[...], by_source)
        back = dot_t(by_source, w_in_ref[latent : 2 * latent])
        low_ref[...] = back[:RIM].astype(BF16)
        high_ref[...] = back[RIM + count :].astype(BF16)
        by_target = by_target_ref[...].astype(BF16)
        total_ref[2 * latent : 3 * latent] = t_dot(node_ref[...], by_target)
        h_ref[...] = (
            partial_ref[...] + back[RIM : RIM + count] + dot_t(by_target, w_in_ref[2 * latent :])
        )
        deal(total_ref, kept_ref, sent_ref, orders[0], parts, me_ref[0])


def node_and_contact(orders, node_parts, contact_parts, row_count, me_ref, host_ref, remote_ref, block_ref, *refs):
    count = 2 * STREAMS * row_count
    far = refs[:count]
    (node_ref, mesh_ref, cot_ref, nw_in_ref, nw_out_ref, cw_in_ref, cw_out_ref,
     out_ref, h_ref, d_mesh_ref, nkept_ref, nsent_ref, ckept_ref, csent_ref,
     *slab_refs) = refs[count : count + 16]
    (x_ref, z_ref, y_ref, sum_ref, total_ref, x_node_ref, d_contact_ref, g_ref,
     nw_in, nw_out, nkept, nsent, sems) = refs[count + 16 :]
    loads = [
        pltpu.make_async_copy(nw_in_ref, nw_in, sems.at[0]),
        pltpu.make_async_copy(nw_out_ref, nw_out, sems.at[1]),
    ]
    stores = [
        pltpu.make_async_copy(nkept, nkept_ref, sems.at[2]),
        pltpu.make_async_copy(nsent, nsent_ref, sems.at[3]),
    ]
    for copy in loads:
        copy.start()
    latent = node_ref.shape[1]
    width = latent // STREAMS
    me = me_ref[0]
    chunk = min(4, row_count)
    blocks = node_ref.shape[0] // BLOCK
    half = nkept_ref.shape[0]

    def own_rows(row):
        return pl.ds(pl.multiple_of(block_ref[row] * BLOCK, BLOCK), BLOCK)

    sum_ref[...] = jnp.zeros_like(sum_ref)
    for row in range(row_count):
        rows = slice(row * BLOCK, (row + 1) * BLOCK)
        x_ref[rows, :latent] = node_ref[own_rows(row), :]
        for s, order in enumerate(orders):
            columns = slice(latent + s * width, latent + (s + 1) * width)
            near, away = far[2 * (row * STREAMS + s)], far[2 * (row * STREAMS + s) + 1]
            is_near = place_of(order, host_ref[row] ^ me) < half

            @pl.when(is_near)
            def _():
                x_ref[rows, columns] = near[0]

            @pl.when(jnp.logical_not(is_near))
            def _():
                x_ref[rows, columns] = away[0]
    for first in range(0, row_count, chunk):
        rows = slice(first * BLOCK, (first + chunk) * BLOCK)
        z = dot(x_ref[rows], cw_in_ref[...])
        y = dot(silu_and_slope(z)[0], cw_out_ref[...])
        z_ref[rows] = z
        y_ref[rows] = y
        message = normed(y)[0].astype(BF16).astype(F32)
        for row in range(first, first + chunk):
            part = message[(row - first) * BLOCK : (row - first + 1) * BLOCK]
            sum_ref[own_rows(row), :] += part

    for copy in loads:
        copy.wait()
    node = node_ref[...]
    x_node_ref[:, :latent] = node
    x_node_ref[:, latent : 2 * latent] = mesh_ref[...]
    x_node_ref[:, 2 * latent :] = sum_ref[...].astype(BF16)
    z = dot(x_node_ref[...], nw_in[...])
    a, slope = silu_and_slope(z)
    y = dot(a, nw_out[...])
    out_ref[...] = (node.astype(F32) + normed(y)[0]).astype(BF16)
    upstream = cot_ref[...].astype(F32)
    d_y = norm_back(y, upstream).astype(BF16)
    total_ref[3 * latent : 4 * latent] = t_dot(a, d_y)
    d_z = (dot_t(d_y, nw_out[...]) * slope).astype(BF16)
    total_ref[: 3 * latent] = t_dot(x_node_ref[...], d_z)
    if total_ref.shape[0] > 4 * latent:
        total_ref[4 * latent :] = jnp.zeros((total_ref.shape[0] - 4 * latent, latent), F32)
    d_x = dot_t(d_z, nw_in[...])
    h_ref[...] = upstream + d_x[:, :latent]
    d_mesh_ref[...] = d_x[:, latent : 2 * latent].astype(BF16)
    d_contact_ref[...] = d_x[:, 2 * latent :].astype(BF16).astype(F32)
    deal(total_ref, nkept, nsent, orders[1], node_parts, me)
    for copy in stores:
        copy.start()

    total_ref[: 3 * latent] = jnp.zeros((3 * latent, latent), F32)
    if total_ref.shape[0] > 3 * latent:
        total_ref[3 * latent :] = jnp.zeros((total_ref.shape[0] - 3 * latent, latent), F32)
    for first in range(0, row_count, chunk):
        rows = slice(first * BLOCK, (first + chunk) * BLOCK)
        for row in range(first, first + chunk):
            part = slice((row - first) * BLOCK, (row - first + 1) * BLOCK)
            g_ref[part, :latent] = d_contact_ref[own_rows(row), :]
        d_y = norm_back(y_ref[rows], g_ref[:, :latent]).astype(BF16)
        a, slope = silu_and_slope(z_ref[rows])
        total_ref[2 * latent : 3 * latent] += t_dot(a, d_y)
        d_z = (dot_t(d_y, cw_out_ref[...]) * slope).astype(BF16)
        total_ref[: 2 * latent] += t_dot(x_ref[rows], d_z)
        g_ref[...] = dot_t(d_z, cw_in_ref[...])
        for row in range(first, first + chunk):
            part = slice((row - first) * BLOCK, (row - first + 1) * BLOCK)
            h_ref[own_rows(row), :] += g_ref[part, :latent]
            label = (host_ref[row] * blocks + remote_ref[row]).astype(F32)
            cut = latent
            for ref in slab_refs:
                columns = ref.shape[2]
                ref[row, :BLOCK] = g_ref[part, cut : cut + columns].astype(BF16)
                ref[row, BLOCK:] = jnp.full((LABEL, columns), label, F32).astype(BF16)
                cut += columns
    deal(total_ref, ckept_ref, csent_ref, orders[2], contact_parts, me)
    for copy in stores:
        copy.wait()


def pick_blocks(orders, blocks, row_count, me_ref, *refs):
    named, quarters, outs, sems = refs[:3], refs[3:9], refs[9:12], refs[12]
    copies = []
    for s, order in enumerate(orders):
        near, away = quarters[2 * s], quarters[2 * s + 1]
        count = near.shape[0]
        for i in range(row_count):
            spot = place_of(order, named[s][i] ^ me_ref[0]) * blocks + named[s][row_count + i]
            spot = jnp.where(spot < 2 * count, spot, 0)
            is_near = spot < count
            sem = sems.at[len(copies)]

            @pl.when(is_near)
            def _():
                pltpu.make_async_copy(near.at[spot], outs[s].at[i], sem).start()

            @pl.when(jnp.logical_not(is_near))
            def _():
                pltpu.make_async_copy(away.at[spot - count], outs[s].at[i], sem).start()

            copies.append(pltpu.make_async_copy(near.at[0], outs[s].at[i], sem))
    for copy in copies:
        copy.wait()


def add_to_places(orders, blocks, half, me_ref, host_ref, remote_ref, *refs):
    own, arrived, outs = refs[:2], refs[2:4], refs[4:]
    row_count = own[0].shape[0]
    width = outs[0].shape[2]
    views = [(0, slice(0, width)), (0, slice(width, 2 * width)), (1, slice(0, width))]
    me = me_ref[0]
    for s, order in enumerate(orders):
        bits = len(order)
        out = outs[s]
        slots = out.shape[0]
        first = half * slots
        array, columns = views[s]
        marks = [arrived[array][i, BLOCK:, columns].astype(F32)[:1] for i in range(row_count)]

        def step(slot, carry):
            place = (first + slot) // blocks
            offset = sum(((place >> (bits - 1 - i)) & 1) << b for i, b in enumerate(order))
            label = ((me ^ offset) * blocks + slot % blocks).astype(F32)
            value = jnp.zeros((BLOCK, out.shape[2]), F32)
            for i, mark in enumerate(marks):
                hit = jnp.where(mark == label, 1.0, 0.0)
                value = value + arrived[array][i, :BLOCK, columns].astype(F32) * hit
            out[slot] = value.astype(out.dtype)
            return carry

        lax.fori_loop(0, slots, step, 0)
        for i in range(row_count):
            spot = place_of(order, host_ref[i] ^ me) * blocks + remote_ref[i] - first

            @pl.when(jnp.logical_and(spot >= 0, spot < slots))
            def _():
                total = out[spot].astype(F32) + own[array][i, :BLOCK, columns].astype(F32)
                out[spot] = total.astype(out.dtype)


def unpack(orders, parts, half_index, me_ref, *refs):
    halves, rest = refs[:STREAMS], refs[STREAMS:]
    outs, rows_refs, sems = rest[-3 * STREAMS - 1 : -STREAMS - 1], rest[-STREAMS - 1 : -1], rest[-1]
    copies = []
    for s, order in enumerate(orders):
        count, width = halves[s].shape[0], halves[s].shape[2]
        rows = halves[s].shape[1] // STREAMS
        for q in range(count):
            for c in range(STREAMS):
                value = halves[s][q, c * rows : (c + 1) * rows].astype(F32)
                rows_refs[s][q, :, c * width : (c + 1) * width] = value
            device = me_ref[0] ^ places(order)[half_index * count + q]
            done = 0
            for p, (_, share) in enumerate(parts[s]):
                start = pl.multiple_of(device * share, 8)
                copy = pltpu.make_async_copy(
                    rows_refs[s].at[q, pl.ds(done, share)],
                    outs[2 * s + p].at[pl.ds(start, share)],
                    sems.at[len(copies)],
                )
                copy.start()
                copies.append(copy)
                done += share
    for copy in copies:
        copy.wait()


def unpack_whole(order, me_ref, near_ref, far_ref, first_ref, second_ref, total_ref):
    half, width = near_ref.shape[0], near_ref.shape[2]
    rows = near_ref.shape[1] // STREAMS
    for q, offset in enumerate(places(order)):
        ref, place = (near_ref, q) if q < half else (far_ref, q - half)
        start = pl.multiple_of((me_ref[0] ^ offset) * rows, 8)
        for s in range(STREAMS):
            value = ref[place, s * rows : (s + 1) * rows].astype(F32)
            total_ref[pl.ds(start, rows), s * width : (s + 1) * width] = value
    cut = first_ref.shape[0]
    first_ref[...] = total_ref[:cut]
    second_ref[...] = total_ref[cut : cut + second_ref.shape[0]]


def params(axes=0):
    return pltpu.CompilerParams(
        vmem_limit_bytes=VMEM_LIMIT,
        dimension_semantics=("arbitrary",) * axes if axes else None,
    )


def cost(flops, moved):
    return pl.CostEstimate(flops=flops, bytes_accessed=moved, transcendentals=0)


def whole(array_shape):
    return pl.BlockSpec(array_shape, lambda *_: (0,) * len(array_shape))


def struct(shape, dtype):
    return jax.ShapeDtypeStruct(shape, dtype)


def on_device(
    node_state,
    edge_state,
    edge_source,
    contact_block,
    contact_host,
    contact_remote,
    w_edge_in,
    w_edge_out,
    w_node_in,
    w_node_out,
    w_contact_in,
    w_contact_out,
    node_cot,
    edge_cot,
):
    node_count, latent = node_state.shape
    edge_count = edge_state.shape[0]
    groups = lax.axis_size("dom")
    blocks = node_count // BLOCK
    row_count = contact_block.shape[0]
    width = latent // STREAMS
    orders = exchange_orders(groups)
    me = lax.axis_index("dom").astype(jnp.int32).reshape(1)
    host = contact_host[:, 0]
    smem = pl.BlockSpec(memory_space=pltpu.SMEM)
    anywhere = pl.BlockSpec(memory_space=pl.ANY)

    inner, outer = swap_rims(node_state[:RIM], node_state[node_count - RIM :])
    last = len(orders[0]) - 1
    far_bit = orders[0][-1]
    half = groups // 2
    rows_named = jnp.concatenate([host, contact_remote])
    arrived, inner, outer, *named = joined(
        [swap(node_state, far_bit), inner, outer]
        + [swap(rows_named, order[0]) for order in orders[:2]]
    )
    before, after = sorted_rims(inner, outer)
    pair = jnp.stack([node_state, arrived])
    slabs = [pair[:, :, s * width : (s + 1) * width] for s in range(STREAMS)]
    for step in range(1, last):
        if step == last - 1:
            *slabs, before, rows_named = joined([*slabs, before, rows_named])
            named.append(swap(rows_named, orders[2][0]))
        arrived = gather_step(slabs, orders, step)
        if step < last - 1:
            slabs = both(slabs, joined(arrived))

    steps = edge_count // EDGE_ROWS
    sources = edge_source.reshape(steps, 1, EDGE_ROWS)
    edge_block = pl.BlockSpec((EDGE_ROWS, latent), lambda i: (i, 0))
    node_block = pl.BlockSpec((EDGE_ROWS // EPN, latent), lambda i: (i, 0))
    source_block = pl.BlockSpec((1, 1, EDGE_ROWS), lambda i: (i, 0, 0))
    rim_block = whole((RIM, latent))
    extended_rows = node_count + 2 * RIM
    edge_out, mesh_sum, e_pre, e_linear = pl.pallas_call(
        edge_forward,
        grid=(steps,),
        in_specs=[
            source_block,
            rim_block,
            whole(node_state.shape),
            rim_block,
            edge_block,
            whole(w_edge_in.shape),
            whole(w_edge_out.shape),
        ],
        out_specs=[edge_block, node_block, edge_block, edge_block],
        out_shape=[
            struct((edge_count, latent), BF16),
            struct((node_count, latent), BF16),
            struct((edge_count, latent), F32),
            struct((edge_count, latent), F32),
        ],
        scratch_shapes=[
            pltpu.VMEM((extended_rows, latent), BF16),
            pltpu.VMEM((EDGE_ROWS, 3 * latent), BF16),
            pltpu.VMEM((EDGE_ROWS, latent), BF16),
        ],
        compiler_params=params(1),
        cost_estimate=cost(2 * edge_count * latent * latent * 6, edge_count * latent * 16),
        name="edge_forward",
    )(sources, before, node_state, after, edge_state, w_edge_in, w_edge_out)

    *arrived, named[2], mesh_sum = joined([*arrived, named[2], mesh_sum])
    quarters = [
        value.reshape(half * blocks // 2, BLOCK, width)
        for pair in zip(slabs, arrived)
        for value in pair
    ]
    picked = pl.pallas_call(
        functools.partial(pick_blocks, orders, blocks, row_count),
        in_specs=[smem] * (1 + STREAMS) + [anywhere] * (2 * STREAMS),
        out_specs=[anywhere] * STREAMS,
        out_shape=[struct((row_count, BLOCK, width), BF16)] * STREAMS,
        scratch_shapes=[pltpu.SemaphoreType.DMA((STREAMS * row_count,))],
        compiler_params=params(),
        cost_estimate=cost(0, 2**20),
        name="pick_blocks",
    )(me, *named, *quarters)
    joined_now = joined([*picked, *quarters])
    picked, quarters = joined_now[:STREAMS], joined_now[STREAMS:]
    slabs = [jnp.concatenate(quarters[2 * s : 2 * s + 2], axis=0) for s in range(STREAMS)]
    answered = [swap(value, order[0]) for value, order in zip(picked, orders)]

    def near_spec(row, s):
        def index(i, me_ref, host_ref, remote_ref, block_ref):
            spot = place_of(orders[s], host_ref[row] ^ me_ref[0])
            return (jnp.where(spot < half, spot * blocks + remote_ref[row], 0), 0, 0)

        return pl.BlockSpec((1, BLOCK, width), index)

    def answer_spec(row):
        return pl.BlockSpec((1, BLOCK, width), lambda *_: (row, 0, 0))

    far = []
    for row in range(row_count):
        for s in range(STREAMS):
            far += [(near_spec(row, s), slabs[s]), (answer_spec(row), answered[s])]
    far_specs, far_args = [spec for spec, _ in far], [arg for _, arg in far]
    matrices = [(w_edge_in, w_edge_out), (w_node_in, w_node_out), (w_contact_in, w_contact_out)]
    parts = [parts_of(first.shape[0], second.shape[0], groups) for first, second in matrices]
    pair_rows = [chunk_rows(part) for part in parts]
    halves = lambda rows: [struct((half, rows * STREAMS, width), BF16)] * 2
    labelled = [
        struct((row_count, BLOCK + LABEL, columns), BF16) for columns in (2 * width, latent - 2 * width)
    ]
    b_out = [
        struct((node_count, latent), BF16),
        struct((node_count, latent), F32),
        struct((node_count, latent), BF16),
        *halves(pair_rows[1]),
        *halves(pair_rows[2]),
        *labelled,
    ]
    b_args = [node_state, mesh_sum, node_cot, w_node_in, w_node_out, w_contact_in, w_contact_out]
    contact_rows = row_count * BLOCK
    chunk_length = min(4, row_count) * BLOCK
    (node_out, partial_h, d_mesh, n_kept, n_sent, c_kept, c_sent, *away) = pl.pallas_call(
        functools.partial(node_and_contact, orders, parts[1], parts[2], row_count),
        grid_spec=pltpu.PrefetchScalarGridSpec(
            num_scalar_prefetch=4,
            grid=(1,),
            in_specs=far_specs
            + [anywhere if 3 <= i <= 4 else whole(arg.shape) for i, arg in enumerate(b_args)],
            out_specs=[
                anywhere if 3 <= i <= 4 else whole(out.shape) for i, out in enumerate(b_out)
            ],
            scratch_shapes=[
                pltpu.VMEM((contact_rows, 2 * latent), BF16),
                pltpu.VMEM((contact_rows, latent), F32),
                pltpu.VMEM((contact_rows, latent), F32),
                pltpu.VMEM((node_count, latent), F32),
                pltpu.VMEM((max(total_rows(part, groups) for part in parts[1:]), latent), F32),
                pltpu.VMEM((node_count, 3 * latent), BF16),
                pltpu.VMEM((node_count, latent), F32),
                pltpu.VMEM((chunk_length, 2 * latent), F32),
                pltpu.VMEM(w_node_in.shape, BF16),
                pltpu.VMEM(w_node_out.shape, BF16),
                pltpu.VMEM(b_out[3].shape, BF16),
                pltpu.VMEM(b_out[4].shape, BF16),
                pltpu.SemaphoreType.DMA((4,)),
            ],
        ),
        out_shape=b_out,
        compiler_params=params(1),
        cost_estimate=cost(2 * (contact_rows * 9 + node_count * 12) * latent * latent, 12 * 2**20),
        name="node_and_contact",
    )(me, host, contact_remote, contact_block, *far_args, *b_args)

    back = return_orders(orders)
    away_arrived = [swap(value, order[0]) for value, order in zip(away, back[1:])]
    n_arrived, c_arrived = swap(n_sent, orders[1][0]), swap(c_sent, orders[2][0])

    edge_grad, near_h, low, high, e_kept, e_sent = pl.pallas_call(
        functools.partial(edge_backward, orders, parts[0]),
        grid=(steps,),
        in_specs=[
            smem,
            source_block,
            rim_block,
            whole(node_state.shape),
            rim_block,
            edge_block,
            edge_block,
            edge_block,
            edge_block,
            node_block,
            whole((node_count, latent)),
            whole(w_edge_in.shape),
            whole(w_edge_out.shape),
        ],
        out_specs=[
            edge_block,
            whole((node_count, latent)),
            rim_block,
            rim_block,
            *[whole((half, pair_rows[0] * STREAMS, width))] * 2,
        ],
        out_shape=[
            struct((edge_count, latent), BF16),
            struct((node_count, latent), F32),
            struct((RIM, latent), BF16),
            struct((RIM, latent), BF16),
            *halves(pair_rows[0]),
        ],
        scratch_shapes=[
            pltpu.VMEM((extended_rows, latent), BF16),
            pltpu.VMEM((extended_rows, latent), F32),
            pltpu.VMEM((node_count, latent), F32),
            pltpu.VMEM((total_rows(parts[0], groups), latent), F32),
        ],
        compiler_params=params(1),
        cost_estimate=cost(2 * edge_count * latent * latent * 8, edge_count * latent * 20),
        name="edge_backward",
    )(me, sources, before, node_state, after, edge_state, e_pre, e_linear, edge_cot, d_mesh,
      partial_h, w_edge_in, w_edge_out)

    *away_arrived, e_sent = joined([*away_arrived, e_sent])
    e_arrived = swap(e_sent, orders[0][0])
    slots = half * blocks // 2
    def places_call(half_index, dtype, own, arrived):
        return pl.pallas_call(
            functools.partial(add_to_places, back, blocks, half_index),
            in_specs=[smem] * 3 + [pl.BlockSpec(memory_space=pltpu.VMEM)] * 4,
            out_specs=[pl.BlockSpec(memory_space=pltpu.VMEM)] * STREAMS,
            out_shape=[struct((slots, BLOCK, width), dtype)] * STREAMS,
            compiler_params=params(),
            cost_estimate=cost(0, 3 * 2**20),
            name="add_to_places",
        )(me, host, contact_remote, *own, *arrived)

    away_sent = places_call(1, BF16, away, away_arrived)
    n_arrived, c_arrived, *away_sent = joined([n_arrived, c_arrived, *away_sent])
    arrived = [swap(sent, order[1]) for sent, order in zip(away_sent, back)]
    arrived[0], *blocks_in = joined([arrived[0], *away, *away_arrived])
    away_kept = places_call(0, F32, blocks_in[:2], blocks_in[2:])
    *arrived, e_arrived = joined([*arrived, e_arrived])
    away = list(zip(away_kept, away_sent))
    away = added(away, arrived)
    weights = added(
        [(e_kept, e_sent), (n_kept, n_sent), (c_kept, c_sent)], [e_arrived, n_arrived, c_arrived]
    )
    for step in range(1, last - 1):
        sent = [jnp.concatenate([a[1], w[1]], axis=1) for a, w in zip(away, weights)]
        arrived = joined([swap(value, order[step]) for value, order in zip(sent, orders)])
        away = added(away, [value[:, :BLOCK] for value in arrived])
        weights = added(weights, [value[:, BLOCK:] for value in arrived])
    arrived = joined([swap(w[1], order[last - 1]) for w, order in zip(weights, orders)])
    mine = jnp.concatenate(
        [(w[0] + value.astype(F32)).astype(BF16) for w, value in zip(weights, arrived)], axis=1
    )
    mine, low, high = joined([mine, low, high])
    theirs, *rims = joined([swap(mine, far_bit), *swap_rims(low, high)])
    high, low = sorted_rims(*rims)
    pair = (mine.astype(F32) + theirs[::-1].astype(F32)).astype(BF16)
    away_sent = jnp.concatenate([sent for _, sent in away], axis=2)
    pair, away_sent = joined([pair, away_sent])
    returned = swap(away_sent, far_bit)
    cuts = [sum(pair_rows[:s]) * STREAMS for s in range(STREAMS + 1)]
    sums = [pair[:, cuts[s] : cuts[s + 1]] for s in range(STREAMS)]
    for step in range(1, last):
        sums = both(sums, joined(gather_step(sums, orders, step)))
    gathered = list(zip(sums, gather_step(sums, orders, last)))
    kept = jnp.concatenate([kept for kept, _ in away], axis=2)
    returned = (kept + returned.astype(F32)).reshape(node_count, latent)
    vmem = pl.BlockSpec(memory_space=pltpu.VMEM)
    if all(len(part) == 2 for part in parts):
        summed = []
        for side in range(2):
            summed = pl.pallas_call(
                functools.partial(unpack, orders, parts, side),
                in_specs=[smem] + [vmem] * STREAMS + [anywhere] * len(summed),
                out_specs=[anywhere] * (2 * STREAMS),
                out_shape=[struct(w.shape, F32) for pair in matrices for w in pair],
                scratch_shapes=[
                    *[pltpu.VMEM((half, rows, latent), F32) for rows in pair_rows],
                    pltpu.SemaphoreType.DMA((2 * STREAMS * half,)),
                ],
                input_output_aliases={1 + STREAMS + i: i for i in range(len(summed))},
                compiler_params=params(),
                cost_estimate=cost(0, half * sum(pair_rows) * latent * 10),
                name="unpack",
            )(me, *[pair[side] for pair in gathered], *summed)
    else:
        summed = []
        for s, (first, second) in enumerate(matrices):
            summed += pl.pallas_call(
                functools.partial(unpack_whole, orders[s]),
                in_specs=[smem] + [vmem] * 2,
                out_specs=[vmem] * 2,
                out_shape=[struct(first.shape, F32), struct(second.shape, F32)],
                scratch_shapes=[pltpu.VMEM((pair_rows[s] * groups, latent), F32)],
                compiler_params=params(),
                name="unpack_whole",
            )(me, *gathered[s])

    rims = jnp.concatenate(
        [
            high.astype(F32),
            jnp.zeros((node_count - 2 * RIM, latent), F32),
            low.astype(F32),
        ],
        axis=0,
    )
    node_grad = (near_h + rims + returned).astype(BF16)
    return (node_out, edge_out, node_grad, edge_grad, *summed)


def solution(mesh):
    rows = P(("rep", "dom"), None)
    flat = P(("rep", "dom"))
    weight = P("rep", None)
    in_specs = (rows, rows, flat, flat, rows, flat) + (weight,) * 6 + (rows, rows)
    out_specs = (rows,) * 4 + (weight,) * 6
    return jax.shard_map(
        on_device, mesh=mesh, in_specs=in_specs, out_specs=out_specs, check_vma=False
    )
```

```python
import functools

import jax
import jax.numpy as jnp
from jax import lax
from jax.experimental import pallas as pl
from jax.experimental.pallas import tpu as pltpu
from jax.sharding import PartitionSpec as P

BLOCK = 128
EPN = 4
RIM = 64
EDGE_ROWS = 512
TILE = 32
STREAMS = 3
VMEM_LIMIT = 50 * 2**20
BF16 = jnp.bfloat16
F32 = jnp.float32


norm_eps = 1e-05


def exchange_orders(groups):
    bits = groups.bit_length() - 1
    low = list(range(bits - 1))
    turns = [r % max(1, len(low)) for r in range(STREAMS)]
    return [low[r:] + low[:r] + [bits - 1] for r in turns]


def return_orders(orders):
    heads = [(o[0], o[-2]) if s == 0 else (o[-2], o[0]) for s, o in enumerate(orders)]
    return [[*head, *o[1:-2], o[-1]] for head, o in zip(heads, orders)]


def places(order):
    bits = len(order)
    return [
        sum(((q >> (bits - 1 - i)) & 1) << b for i, b in enumerate(order)) for q in range(1 << bits)
    ]


def place_of(order, offset):
    bits = len(order)
    return sum(((offset >> b) & 1) << (bits - 1 - i) for i, b in enumerate(order))


def swap(value, bit):
    peers = lax.axis_size("dom")
    return lax.ppermute(value, "dom", [(i, i ^ (1 << bit)) for i in range(peers)])


def swap_rims(first, last):
    peers = lax.axis_size("dom")
    odd = lax.axis_index("dom") % 2 == 1
    pairs = [[(i, i + 1) for i in range(start, peers - 1, 2)] for start in range(2)]
    both_ways = [pair + [(j, i) for i, j in pair] for pair in pairs]
    inner = lax.ppermute(jnp.where(odd, first, last), "dom", both_ways[0])
    outer = lax.ppermute(jnp.where(odd, last, first), "dom", both_ways[1])
    return inner, outer


def sorted_rims(inner, outer):
    odd = lax.axis_index("dom") % 2 == 1
    return jnp.where(odd, inner, outer), jnp.where(odd, outer, inner)


def joined(values):
    return list(lax.optimization_barrier(tuple(values)))


def gather_step(held, orders, step):
    return [swap(value, order[-1 - step]) for value, order in zip(held, orders)]


def both(held, arrived):
    return [jnp.concatenate(pair, axis=0) for pair in zip(held, arrived)]


def added(halves, arrived):
    totals = [kept.astype(F32) + value.astype(F32) for (kept, _), value in zip(halves, arrived)]
    cut = totals[0].shape[0] // 2
    return [(total[:cut], total[cut:].astype(BF16)) for total in totals]


def dot(a, b):
    return jnp.dot(a, b, preferred_element_type=F32)


def dot_t(a, b):
    return lax.dot_general(a, b, (((1,), (1,)), ((), ())), preferred_element_type=F32)


def t_dot(a, b):
    return lax.dot_general(a, b, (((0,), (0,)), ((), ())), preferred_element_type=F32)


def sigmoid(z):
    return 0.5 * jnp.tanh(0.5 * z) + 0.5


def normed(values):
    center = values - jnp.mean(values, axis=-1, keepdims=True)
    scale = lax.rsqrt(jnp.mean(center * center, axis=-1, keepdims=True) + norm_eps)
    return center * scale, scale


def norm_back(values, upstream):
    unit, scale = normed(values)
    first = jnp.mean(upstream, axis=-1, keepdims=True)
    second = jnp.mean(upstream * unit, axis=-1, keepdims=True)
    return scale * (upstream - first - unit * second)


def tiles(rows):
    return [slice(i, i + TILE) for i in range(0, rows, TILE)]


def silu_tiles(z_ref, a_ref):
    for t in tiles(z_ref.shape[0]):
        z = z_ref[t]
        a_ref[t] = (z * sigmoid(z)).astype(BF16)


def silu_and_slope(z):
    s = sigmoid(z)
    a = z * s
    return a.astype(BF16), s + a * (1.0 - s)


def one_hot(condition):
    return jnp.where(condition, 1.0, 0.0).astype(BF16)


def iota(shape, axis):
    return lax.broadcasted_iota(jnp.int32, shape, axis)


def repeat_matrix(rows):
    shape = (rows, rows // EPN)
    return one_hot((iota(shape, 0) >> 2) == iota(shape, 1))


def sum_matrix(rows):
    shape = (rows // EPN, rows)
    return one_hot((iota(shape, 1) >> 2) == iota(shape, 0))


def parts_of(first, second, groups):
    shares = first // groups, second // groups
    if all(share % 8 == 0 and share * groups == size for share, size in zip(shares, (first, second))):
        return [(0, shares[0]), (first, shares[1])]
    return [(0, -(-(first + second) // (groups * 16)) * 16)]


def chunk_rows(parts):
    return -(-sum(rows for _, rows in parts) // 16) * 16


def total_rows(parts, groups):
    return max(base + rows * groups for base, rows in parts)


def starts_of(parts, device):
    return [pl.multiple_of(base + device * rows, 8) for base, rows in parts]


def deal(total_ref, kept_ref, sent_ref, order, parts, me):
    half, width = kept_ref.shape[0], kept_ref.shape[2]
    rows = kept_ref.shape[1] // STREAMS
    spare = rows - sum(count for _, count in parts)
    for q, offset in enumerate(places(order)):
        starts = starts_of(parts, me ^ offset)
        for s in range(STREAMS):
            columns = slice(s * width, (s + 1) * width)
            values = [
                total_ref[pl.ds(start, count), columns] for start, (_, count) in zip(starts, parts)
            ]
            if spare:
                values.append(jnp.zeros((spare, width), F32))
            value = jnp.concatenate(values, axis=0) if len(values) > 1 else values[0]
            if q < half:
                kept_ref[q, s * rows : (s + 1) * rows] = value.astype(kept_ref.dtype)
            else:
                sent_ref[q - half, s * rows : (s + 1) * rows] = value.astype(BF16)


def edge_forward(src_ref, before_ref, node_ref, after_ref, edge_ref, w_in_ref, w_out_ref,
                 out_ref, sum_ref, z_ref, y_ref, ext_ref, x_ref, a_ref):
    step = pl.program_id(0)
    count, latent = node_ref.shape
    rows = edge_ref.shape[0]
    targets = rows // EPN

    @pl.when(step == 0)
    def _():
        ext_ref[:RIM] = before_ref[...]
        ext_ref[RIM : RIM + count] = node_ref[...]
        ext_ref[RIM + count :] = after_ref[...]

    hit = one_hot(iota((count + 2 * RIM, rows), 0) == src_ref[0])
    own = node_ref[pl.ds(pl.multiple_of(step * targets, targets), targets), :]
    x_ref[:, :latent] = edge_ref[...]
    x_ref[:, latent : 2 * latent] = t_dot(hit, ext_ref[...]).astype(BF16)
    x_ref[:, 2 * latent :] = dot(repeat_matrix(rows), own).astype(BF16)
    z_ref[...] = dot(x_ref[...], w_in_ref[...])
    silu_tiles(z_ref, a_ref)
    y_ref[...] = dot(a_ref[...], w_out_ref[...])
    for t in tiles(rows):
        out_ref[t] = (edge_ref[t].astype(F32) + normed(y_ref[t])[0]).astype(BF16)
    sum_ref[...] = dot(sum_matrix(rows), out_ref[...]).astype(BF16)


def edge_backward(orders, parts, me_ref, src_ref, before_ref, node_ref, after_ref, edge_ref, z_ref, y_ref,
                  cot_ref, mesh_ref, partial_ref, w_in_ref, w_out_ref,
                  grad_ref, h_ref, low_ref, high_ref, kept_ref, sent_ref,
                  ext_ref, by_source_ref, by_target_ref, total_ref):
    step = pl.program_id(0)
    count, latent = node_ref.shape
    rows = edge_ref.shape[0]
    targets = rows // EPN

    @pl.when(step == 0)
    def _():
        by_source_ref[...] = jnp.zeros_like(by_source_ref)
        total_ref[...] = jnp.zeros_like(total_ref)

    upstream = cot_ref[...].astype(F32) + dot(repeat_matrix(rows), mesh_ref[...])
    d_y = norm_back(y_ref[...], upstream).astype(BF16)
    a, slope = silu_and_slope(z_ref[...])
    total_ref[3 * latent : 4 * latent] += t_dot(a, d_y)
    d_z = (dot_t(d_y, w_out_ref[...]) * slope).astype(BF16)
    total_ref[:latent] += t_dot(edge_ref[...], d_z)
    grad_ref[...] = (upstream + dot_t(d_z, w_in_ref[:latent])).astype(BF16)
    hit = one_hot(iota((count + 2 * RIM, rows), 0) == src_ref[0])
    by_source_ref[...] += dot(hit, d_z)
    place = pl.ds(pl.multiple_of(step * targets, targets), targets)
    by_target_ref[place, :] = dot(sum_matrix(rows), d_z)

    @pl.when(step == pl.num_programs(0) - 1)
    def _():
        ext_ref[:RIM] = before_ref[...]
        ext_ref[RIM : RIM + count] = node_ref[...]
        ext_ref[RIM + count :] = after_ref[...]
        by_source = by_source_ref[...].astype(BF16)
        total_ref[latent : 2 * latent] = t_dot(ext_ref[...], by_source)
        back = dot_t(by_source, w_in_ref[latent : 2 * latent])
        low_ref[...] = back[:RIM].astype(BF16)
        high_ref[...] = back[RIM + count :].astype(BF16)
        by_target = by_target_ref[...].astype(BF16)
        total_ref[2 * latent : 3 * latent] = t_dot(node_ref[...], by_target)
        h_ref[...] = (
            partial_ref[...] + back[RIM : RIM + count] + dot_t(by_target, w_in_ref[2 * latent :])
        )
        deal(total_ref, kept_ref, sent_ref, orders[0], parts, me_ref[0])


def node_and_contact(orders, node_parts, contact_parts, row_count, me_ref, host_ref, remote_ref, block_ref, *refs):
    count = 2 * STREAMS * row_count
    far = refs[:count]
    (node_ref, mesh_ref, cot_ref, nw_in_ref, nw_out_ref, cw_in_ref, cw_out_ref,
     out_ref, h_ref, d_mesh_ref, nkept_ref, nsent_ref, ckept_ref, csent_ref,
     *slab_refs) = refs[count : count + 16]
    (x_ref, z_ref, y_ref, sum_ref, total_ref, x_node_ref, d_contact_ref, g_ref,
     nw_in, nw_out, nkept, nsent, sems) = refs[count + 16 :]
    loads = [
        pltpu.make_async_copy(nw_in_ref, nw_in, sems.at[0]),
        pltpu.make_async_copy(nw_out_ref, nw_out, sems.at[1]),
    ]
    stores = [
        pltpu.make_async_copy(nkept, nkept_ref, sems.at[2]),
        pltpu.make_async_copy(nsent, nsent_ref, sems.at[3]),
    ]
    for copy in loads:
        copy.start()
    latent = node_ref.shape[1]
    width = latent // STREAMS
    me = me_ref[0]
    chunk = min(4, row_count)
    blocks = node_ref.shape[0] // BLOCK
    half = nkept_ref.shape[0]

    def own_rows(row):
        return pl.ds(pl.multiple_of(block_ref[row] * BLOCK, BLOCK), BLOCK)

    sum_ref[...] = jnp.zeros_like(sum_ref)
    for row in range(row_count):
        rows = slice(row * BLOCK, (row + 1) * BLOCK)
        x_ref[rows, :latent] = node_ref[own_rows(row), :]
        for s, order in enumerate(orders):
            columns = slice(latent + s * width, latent + (s + 1) * width)
            near, away = far[2 * (row * STREAMS + s)], far[2 * (row * STREAMS + s) + 1]
            is_near = place_of(order, host_ref[row] ^ me) < half

            @pl.when(is_near)
            def _():
                x_ref[rows, columns] = near[0]

            @pl.when(jnp.logical_not(is_near))
            def _():
                x_ref[rows, columns] = away[0]
    for first in range(0, row_count, chunk):
        rows = slice(first * BLOCK, (first + chunk) * BLOCK)
        z = dot(x_ref[rows], cw_in_ref[...])
        y = dot(silu_and_slope(z)[0], cw_out_ref[...])
        z_ref[rows] = z
        y_ref[rows] = y
        message = normed(y)[0].astype(BF16).astype(F32)
        for row in range(first, first + chunk):
            part = message[(row - first) * BLOCK : (row - first + 1) * BLOCK]
            sum_ref[own_rows(row), :] += part

    for copy in loads:
        copy.wait()
    node = node_ref[...]
    x_node_ref[:, :latent] = node
    x_node_ref[:, latent : 2 * latent] = mesh_ref[...]
    x_node_ref[:, 2 * latent :] = sum_ref[...].astype(BF16)
    z = dot(x_node_ref[...], nw_in[...])
    a, slope = silu_and_slope(z)
    y = dot(a, nw_out[...])
    out_ref[...] = (node.astype(F32) + normed(y)[0]).astype(BF16)
    upstream = cot_ref[...].astype(F32)
    d_y = norm_back(y, upstream).astype(BF16)
    total_ref[3 * latent : 4 * latent] = t_dot(a, d_y)
    d_z = (dot_t(d_y, nw_out[...]) * slope).astype(BF16)
    total_ref[: 3 * latent] = t_dot(x_node_ref[...], d_z)
    if total_ref.shape[0] > 4 * latent:
        total_ref[4 * latent :] = jnp.zeros((total_ref.shape[0] - 4 * latent, latent), F32)
    d_x = dot_t(d_z, nw_in[...])
    h_ref[...] = upstream + d_x[:, :latent]
    d_mesh_ref[...] = d_x[:, latent : 2 * latent].astype(BF16)
    d_contact_ref[...] = d_x[:, 2 * latent :].astype(BF16).astype(F32)
    deal(total_ref, nkept, nsent, orders[1], node_parts, me)
    for copy in stores:
        copy.start()

    total_ref[: 3 * latent] = jnp.zeros((3 * latent, latent), F32)
    if total_ref.shape[0] > 3 * latent:
        total_ref[3 * latent :] = jnp.zeros((total_ref.shape[0] - 3 * latent, latent), F32)
    for first in range(0, row_count, chunk):
        rows = slice(first * BLOCK, (first + chunk) * BLOCK)
        for row in range(first, first + chunk):
            part = slice((row - first) * BLOCK, (row - first + 1) * BLOCK)
            g_ref[part, :latent] = d_contact_ref[own_rows(row), :]
        d_y = norm_back(y_ref[rows], g_ref[:, :latent]).astype(BF16)
        a, slope = silu_and_slope(z_ref[rows])
        total_ref[2 * latent : 3 * latent] += t_dot(a, d_y)
        d_z = (dot_t(d_y, cw_out_ref[...]) * slope).astype(BF16)
        total_ref[: 2 * latent] += t_dot(x_ref[rows], d_z)
        g_ref[...] = dot_t(d_z, cw_in_ref[...])
        for row in range(first, first + chunk):
            part = slice((row - first) * BLOCK, (row - first + 1) * BLOCK)
            h_ref[own_rows(row), :] += g_ref[part, :latent]
            cut = latent
            for ref in slab_refs:
                columns = ref.shape[2]
                ref[row] = g_ref[part, cut : cut + columns].astype(BF16)
                cut += columns
    deal(total_ref, ckept_ref, csent_ref, orders[2], contact_parts, me)
    for copy in stores:
        copy.wait()


def pick_blocks(orders, blocks, row_count, me_ref, *refs):
    named, quarters, outs, sems = refs[:3], refs[3:9], refs[9:12], refs[12]
    copies = []
    for s, order in enumerate(orders):
        near, away = quarters[2 * s], quarters[2 * s + 1]
        count = near.shape[0]
        for i in range(row_count):
            spot = place_of(order, named[s][i] ^ me_ref[0]) * blocks + named[s][row_count + i]
            spot = jnp.where(spot < 2 * count, spot, 0)
            is_near = spot < count
            sem = sems.at[len(copies)]

            @pl.when(is_near)
            def _():
                pltpu.make_async_copy(near.at[spot], outs[s].at[i], sem).start()

            @pl.when(jnp.logical_not(is_near))
            def _():
                pltpu.make_async_copy(away.at[spot - count], outs[s].at[i], sem).start()

            copies.append(pltpu.make_async_copy(near.at[0], outs[s].at[i], sem))
    for copy in copies:
        copy.wait()


def add_to_places(orders, blocks, half, me_ref, host_ref, remote_ref, *refs):
    named, own, arrived, outs = refs[:2], refs[2:4], refs[4:6], refs[6:]
    row_count = own[0].shape[0]
    width = outs[0].shape[2]
    views = [(0, slice(0, width)), (0, slice(width, 2 * width)), (1, slice(0, width))]
    me = me_ref[0]
    for s, order in enumerate(orders):
        out = outs[s]
        slots = out.shape[0]
        array, columns = views[s]
        out[...] = jnp.zeros_like(out)

        def place(source, i, host, remote):
            spot = place_of(order, host ^ me) * blocks + remote - half * slots

            @pl.when(jnp.logical_and(spot >= 0, spot < slots))
            def _():
                total = out[spot].astype(F32) + source[array][i, :, columns].astype(F32)
                out[spot] = total.astype(out.dtype)

        for i in range(row_count):
            place(own, i, host_ref[i], remote_ref[i])
            place(arrived, i, named[array][i], named[array][row_count + i])


def unpack(orders, parts, half_index, me_ref, *refs):
    halves, rest = refs[:STREAMS], refs[STREAMS:]
    outs, rows_refs, sems = rest[-3 * STREAMS - 1 : -STREAMS - 1], rest[-STREAMS - 1 : -1], rest[-1]
    copies = []
    for s, order in enumerate(orders):
        count, width = halves[s].shape[0], halves[s].shape[2]
        rows = halves[s].shape[1] // STREAMS
        for q in range(count):
            for c in range(STREAMS):
                value = halves[s][q, c * rows : (c + 1) * rows].astype(F32)
                rows_refs[s][q, :, c * width : (c + 1) * width] = value
            device = me_ref[0] ^ places(order)[half_index * count + q]
            done = 0
            for p, (_, share) in enumerate(parts[s]):
                start = pl.multiple_of(device * share, 8)
                copy = pltpu.make_async_copy(
                    rows_refs[s].at[q, pl.ds(done, share)],
                    outs[2 * s + p].at[pl.ds(start, share)],
                    sems.at[len(copies)],
                )
                copy.start()
                copies.append(copy)
                done += share
    for copy in copies:
        copy.wait()


def unpack_whole(order, me_ref, near_ref, far_ref, first_ref, second_ref, total_ref):
    half, width = near_ref.shape[0], near_ref.shape[2]
    rows = near_ref.shape[1] // STREAMS
    for q, offset in enumerate(places(order)):
        ref, place = (near_ref, q) if q < half else (far_ref, q - half)
        start = pl.multiple_of((me_ref[0] ^ offset) * rows, 8)
        for s in range(STREAMS):
            value = ref[place, s * rows : (s + 1) * rows].astype(F32)
            total_ref[pl.ds(start, rows), s * width : (s + 1) * width] = value
    cut = first_ref.shape[0]
    first_ref[...] = total_ref[:cut]
    second_ref[...] = total_ref[cut : cut + second_ref.shape[0]]


def params(axes=0):
    return pltpu.CompilerParams(
        vmem_limit_bytes=VMEM_LIMIT,
        dimension_semantics=("arbitrary",) * axes if axes else None,
    )


def cost(flops, moved):
    return pl.CostEstimate(flops=flops, bytes_accessed=moved, transcendentals=0)


def whole(array_shape):
    return pl.BlockSpec(array_shape, lambda *_: (0,) * len(array_shape))


def struct(shape, dtype):
    return jax.ShapeDtypeStruct(shape, dtype)


def on_device(
    node_state,
    edge_state,
    edge_source,
    contact_block,
    contact_host,
    contact_remote,
    w_edge_in,
    w_edge_out,
    w_node_in,
    w_node_out,
    w_contact_in,
    w_contact_out,
    node_cot,
    edge_cot,
):
    node_count, latent = node_state.shape
    edge_count = edge_state.shape[0]
    groups = lax.axis_size("dom")
    blocks = node_count // BLOCK
    row_count = contact_block.shape[0]
    width = latent // STREAMS
    orders = exchange_orders(groups)
    me = lax.axis_index("dom").astype(jnp.int32).reshape(1)
    host = contact_host[:, 0]
    smem = pl.BlockSpec(memory_space=pltpu.SMEM)
    anywhere = pl.BlockSpec(memory_space=pl.ANY)

    inner, outer = swap_rims(node_state[:RIM], node_state[node_count - RIM :])
    last = len(orders[0]) - 1
    far_bit = orders[0][-1]
    half = groups // 2
    rows_named = jnp.concatenate([host, contact_remote])
    arrived, inner, outer, *named = joined(
        [swap(node_state, far_bit), inner, outer]
        + [swap(rows_named, order[0]) for order in orders[:2]]
    )
    before, after = sorted_rims(inner, outer)
    pair = jnp.stack([node_state, arrived])
    slabs = [pair[:, :, s * width : (s + 1) * width] for s in range(STREAMS)]
    for step in range(1, last):
        if step == last - 1:
            *slabs, before, rows_named = joined([*slabs, before, rows_named])
            named.append(swap(rows_named, orders[2][0]))
        arrived = gather_step(slabs, orders, step)
        if step < last - 1:
            slabs = both(slabs, joined(arrived))

    steps = edge_count // EDGE_ROWS
    sources = edge_source.reshape(steps, 1, EDGE_ROWS)
    edge_block = pl.BlockSpec((EDGE_ROWS, latent), lambda i: (i, 0))
    node_block = pl.BlockSpec((EDGE_ROWS // EPN, latent), lambda i: (i, 0))
    source_block = pl.BlockSpec((1, 1, EDGE_ROWS), lambda i: (i, 0, 0))
    rim_block = whole((RIM, latent))
    extended_rows = node_count + 2 * RIM
    edge_out, mesh_sum, e_pre, e_linear = pl.pallas_call(
        edge_forward,
        grid=(steps,),
        in_specs=[
            source_block,
            rim_block,
            whole(node_state.shape),
            rim_block,
            edge_block,
            whole(w_edge_in.shape),
            whole(w_edge_out.shape),
        ],
        out_specs=[edge_block, node_block, edge_block, edge_block],
        out_shape=[
            struct((edge_count, latent), BF16),
            struct((node_count, latent), BF16),
            struct((edge_count, latent), F32),
            struct((edge_count, latent), F32),
        ],
        scratch_shapes=[
            pltpu.VMEM((extended_rows, latent), BF16),
            pltpu.VMEM((EDGE_ROWS, 3 * latent), BF16),
            pltpu.VMEM((EDGE_ROWS, latent), BF16),
        ],
        compiler_params=params(1),
        cost_estimate=cost(2 * edge_count * latent * latent * 6, edge_count * latent * 16),
        name="edge_forward",
    )(sources, before, node_state, after, edge_state, w_edge_in, w_edge_out)

    *arrived, named[2], mesh_sum = joined([*arrived, named[2], mesh_sum])
    quarters = [
        value.reshape(half * blocks // 2, BLOCK, width)
        for pair in zip(slabs, arrived)
        for value in pair
    ]
    picked = pl.pallas_call(
        functools.partial(pick_blocks, orders, blocks, row_count),
        in_specs=[smem] * (1 + STREAMS) + [anywhere] * (2 * STREAMS),
        out_specs=[anywhere] * STREAMS,
        out_shape=[struct((row_count, BLOCK, width), BF16)] * STREAMS,
        scratch_shapes=[pltpu.SemaphoreType.DMA((STREAMS * row_count,))],
        compiler_params=params(),
        cost_estimate=cost(0, 2**20),
        name="pick_blocks",
    )(me, *named, *quarters)
    joined_now = joined([*picked, *quarters])
    picked, quarters = joined_now[:STREAMS], joined_now[STREAMS:]
    slabs = [jnp.concatenate(quarters[2 * s : 2 * s + 2], axis=0) for s in range(STREAMS)]
    answered = [swap(value, order[0]) for value, order in zip(picked, orders)]

    def near_spec(row, s):
        def index(i, me_ref, host_ref, remote_ref, block_ref):
            spot = place_of(orders[s], host_ref[row] ^ me_ref[0])
            return (jnp.where(spot < half, spot * blocks + remote_ref[row], 0), 0, 0)

        return pl.BlockSpec((1, BLOCK, width), index)

    def answer_spec(row):
        return pl.BlockSpec((1, BLOCK, width), lambda *_: (row, 0, 0))

    far = []
    for row in range(row_count):
        for s in range(STREAMS):
            far += [(near_spec(row, s), slabs[s]), (answer_spec(row), answered[s])]
    far_specs, far_args = [spec for spec, _ in far], [arg for _, arg in far]
    matrices = [(w_edge_in, w_edge_out), (w_node_in, w_node_out), (w_contact_in, w_contact_out)]
    parts = [parts_of(first.shape[0], second.shape[0], groups) for first, second in matrices]
    pair_rows = [chunk_rows(part) for part in parts]
    halves = lambda rows: [struct((half, rows * STREAMS, width), BF16)] * 2
    remote_parts = [
        struct((row_count, BLOCK, columns), BF16) for columns in (2 * width, latent - 2 * width)
    ]
    b_out = [
        struct((node_count, latent), BF16),
        struct((node_count, latent), F32),
        struct((node_count, latent), BF16),
        *halves(pair_rows[1]),
        *halves(pair_rows[2]),
        *remote_parts,
    ]
    b_args = [node_state, mesh_sum, node_cot, w_node_in, w_node_out, w_contact_in, w_contact_out]
    contact_rows = row_count * BLOCK
    chunk_length = min(4, row_count) * BLOCK
    (node_out, partial_h, d_mesh, n_kept, n_sent, c_kept, c_sent, *away) = pl.pallas_call(
        functools.partial(node_and_contact, orders, parts[1], parts[2], row_count),
        grid_spec=pltpu.PrefetchScalarGridSpec(
            num_scalar_prefetch=4,
            grid=(1,),
            in_specs=far_specs
            + [anywhere if 3 <= i <= 4 else whole(arg.shape) for i, arg in enumerate(b_args)],
            out_specs=[
                anywhere if 3 <= i <= 4 else whole(out.shape) for i, out in enumerate(b_out)
            ],
            scratch_shapes=[
                pltpu.VMEM((contact_rows, 2 * latent), BF16),
                pltpu.VMEM((contact_rows, latent), F32),
                pltpu.VMEM((contact_rows, latent), F32),
                pltpu.VMEM((node_count, latent), F32),
                pltpu.VMEM((max(total_rows(part, groups) for part in parts[1:]), latent), F32),
                pltpu.VMEM((node_count, 3 * latent), BF16),
                pltpu.VMEM((node_count, latent), F32),
                pltpu.VMEM((chunk_length, 2 * latent), F32),
                pltpu.VMEM(w_node_in.shape, BF16),
                pltpu.VMEM(w_node_out.shape, BF16),
                pltpu.VMEM(b_out[3].shape, BF16),
                pltpu.VMEM(b_out[4].shape, BF16),
                pltpu.SemaphoreType.DMA((4,)),
            ],
        ),
        out_shape=b_out,
        compiler_params=params(1),
        cost_estimate=cost(2 * (contact_rows * 9 + node_count * 12) * latent * latent, 12 * 2**20),
        name="node_and_contact",
    )(me, host, contact_remote, contact_block, *far_args, *b_args)

    back = return_orders(orders)
    away_arrived = [swap(value, order[0]) for value, order in zip(away, back[1:])]
    n_arrived, c_arrived = swap(n_sent, orders[1][0]), swap(c_sent, orders[2][0])

    edge_grad, near_h, low, high, e_kept, e_sent = pl.pallas_call(
        functools.partial(edge_backward, orders, parts[0]),
        grid=(steps,),
        in_specs=[
            smem,
            source_block,
            rim_block,
            whole(node_state.shape),
            rim_block,
            edge_block,
            edge_block,
            edge_block,
            edge_block,
            node_block,
            whole((node_count, latent)),
            whole(w_edge_in.shape),
            whole(w_edge_out.shape),
        ],
        out_specs=[
            edge_block,
            whole((node_count, latent)),
            rim_block,
            rim_block,
            *[whole((half, pair_rows[0] * STREAMS, width))] * 2,
        ],
        out_shape=[
            struct((edge_count, latent), BF16),
            struct((node_count, latent), F32),
            struct((RIM, latent), BF16),
            struct((RIM, latent), BF16),
            *halves(pair_rows[0]),
        ],
        scratch_shapes=[
            pltpu.VMEM((extended_rows, latent), BF16),
            pltpu.VMEM((extended_rows, latent), F32),
            pltpu.VMEM((node_count, latent), F32),
            pltpu.VMEM((total_rows(parts[0], groups), latent), F32),
        ],
        compiler_params=params(1),
        cost_estimate=cost(2 * edge_count * latent * latent * 8, edge_count * latent * 20),
        name="edge_backward",
    )(me, sources, before, node_state, after, edge_state, e_pre, e_linear, edge_cot, d_mesh,
      partial_h, w_edge_in, w_edge_out)

    *away_arrived, e_sent = joined([*away_arrived, e_sent])
    e_arrived = swap(e_sent, orders[0][0])
    slots = half * blocks // 2
    def places_call(half_index, dtype, own, arrived):
        return pl.pallas_call(
            functools.partial(add_to_places, back, blocks, half_index),
            in_specs=[smem] * 5 + [pl.BlockSpec(memory_space=pltpu.VMEM)] * 4,
            out_specs=[pl.BlockSpec(memory_space=pltpu.VMEM)] * STREAMS,
            out_shape=[struct((slots, BLOCK, width), dtype)] * STREAMS,
            compiler_params=params(),
            cost_estimate=cost(0, 3 * 2**20),
            name="add_to_places",
        )(me, host, contact_remote, *named[:2], *own, *arrived)

    away_sent = places_call(1, BF16, away, away_arrived)
    n_arrived, c_arrived, *away_sent = joined([n_arrived, c_arrived, *away_sent])
    arrived = [swap(sent, order[1]) for sent, order in zip(away_sent, back)]
    arrived[0], *blocks_in = joined([arrived[0], *away, *away_arrived])
    away_kept = places_call(0, F32, blocks_in[:2], blocks_in[2:])
    *arrived, e_arrived = joined([*arrived, e_arrived])
    away = list(zip(away_kept, away_sent))
    away = added(away, arrived)
    weights = added(
        [(e_kept, e_sent), (n_kept, n_sent), (c_kept, c_sent)], [e_arrived, n_arrived, c_arrived]
    )
    for step in range(1, last - 1):
        sent = [jnp.concatenate([a[1], w[1]], axis=1) for a, w in zip(away, weights)]
        arrived = joined([swap(value, order[step]) for value, order in zip(sent, orders)])
        away = added(away, [value[:, :BLOCK] for value in arrived])
        weights = added(weights, [value[:, BLOCK:] for value in arrived])
    arrived = joined([swap(w[1], order[last - 1]) for w, order in zip(weights, orders)])
    mine = jnp.concatenate(
        [(w[0] + value.astype(F32)).astype(BF16) for w, value in zip(weights, arrived)], axis=1
    )
    mine, low, high = joined([mine, low, high])
    theirs, *rims = joined([swap(mine, far_bit), *swap_rims(low, high)])
    high, low = sorted_rims(*rims)
    pair = (mine.astype(F32) + theirs[::-1].astype(F32)).astype(BF16)
    away_sent = jnp.concatenate([sent for _, sent in away], axis=2)
    pair, away_sent = joined([pair, away_sent])
    returned = swap(away_sent, far_bit)
    cuts = [sum(pair_rows[:s]) * STREAMS for s in range(STREAMS + 1)]
    sums = [pair[:, cuts[s] : cuts[s + 1]] for s in range(STREAMS)]
    for step in range(1, last):
        sums = both(sums, joined(gather_step(sums, orders, step)))
    gathered = list(zip(sums, gather_step(sums, orders, last)))
    kept = jnp.concatenate([kept for kept, _ in away], axis=2)
    returned = (kept + returned.astype(F32)).reshape(node_count, latent)
    vmem = pl.BlockSpec(memory_space=pltpu.VMEM)
    if all(len(part) == 2 for part in parts):
        summed = []
        for side in range(2):
            summed = pl.pallas_call(
                functools.partial(unpack, orders, parts, side),
                in_specs=[smem] + [vmem] * STREAMS + [anywhere] * len(summed),
                out_specs=[anywhere] * (2 * STREAMS),
                out_shape=[struct(w.shape, F32) for pair in matrices for w in pair],
                scratch_shapes=[
                    *[pltpu.VMEM((half, rows, latent), F32) for rows in pair_rows],
                    pltpu.SemaphoreType.DMA((2 * STREAMS * half,)),
                ],
                input_output_aliases={1 + STREAMS + i: i for i in range(len(summed))},
                compiler_params=params(),
                cost_estimate=cost(0, half * sum(pair_rows) * latent * 10),
                name="unpack",
            )(me, *[pair[side] for pair in gathered], *summed)
    else:
        summed = []
        for s, (first, second) in enumerate(matrices):
            summed += pl.pallas_call(
                functools.partial(unpack_whole, orders[s]),
                in_specs=[smem] + [vmem] * 2,
                out_specs=[vmem] * 2,
                out_shape=[struct(first.shape, F32), struct(second.shape, F32)],
                scratch_shapes=[pltpu.VMEM((pair_rows[s] * groups, latent), F32)],
                compiler_params=params(),
                name="unpack_whole",
            )(me, *gathered[s])

    rims = jnp.concatenate(
        [
            high.astype(F32),
            jnp.zeros((node_count - 2 * RIM, latent), F32),
            low.astype(F32),
        ],
        axis=0,
    )
    node_grad = (near_h + rims + returned).astype(BF16)
    return (node_out, edge_out, node_grad, edge_grad, *summed)


def solution(mesh):
    rows = P(("rep", "dom"), None)
    flat = P(("rep", "dom"))
    weight = P("rep", None)
    in_specs = (rows, rows, flat, flat, rows, flat) + (weight,) * 6 + (rows, rows)
    out_specs = (rows,) * 4 + (weight,) * 6
    return jax.shard_map(
        on_device, mesh=mesh, in_specs=in_specs, out_specs=out_specs, check_vma=False
    )
```

```python
import functools

import jax
import jax.numpy as jnp
from jax import lax
from jax.experimental import pallas as pl
from jax.experimental.pallas import tpu as pltpu
from jax.sharding import PartitionSpec as P

BLOCK = 128
EPN = 4
RIM = 64
EDGE_ROWS = 512
TILE = 32
STREAMS = 3
VMEM_LIMIT = 50 * 2**20
BF16 = jnp.bfloat16
F32 = jnp.float32


norm_eps = 1e-05


def exchange_orders(groups):
    bits = groups.bit_length() - 1
    low = list(range(bits - 1))
    turns = [r % max(1, len(low)) for r in range(STREAMS)]
    return [low[r:] + low[:r] + [bits - 1] for r in turns]


def return_orders(orders):
    heads = [(o[0], o[-2]) if s == 0 else (o[-2], o[0]) for s, o in enumerate(orders)]
    return [[*head, *o[1:-2], o[-1]] for head, o in zip(heads, orders)]


def places(order):
    bits = len(order)
    return [
        sum(((q >> (bits - 1 - i)) & 1) << b for i, b in enumerate(order)) for q in range(1 << bits)
    ]


def place_of(order, offset):
    bits = len(order)
    return sum(((offset >> b) & 1) << (bits - 1 - i) for i, b in enumerate(order))


def swap(value, bit):
    peers = lax.axis_size("dom")
    return lax.ppermute(value, "dom", [(i, i ^ (1 << bit)) for i in range(peers)])


def swap_rims(first, last):
    peers = lax.axis_size("dom")
    odd = lax.axis_index("dom") % 2 == 1
    pairs = [[(i, i + 1) for i in range(start, peers - 1, 2)] for start in range(2)]
    both_ways = [pair + [(j, i) for i, j in pair] for pair in pairs]
    inner = lax.ppermute(jnp.where(odd, first, last), "dom", both_ways[0])
    outer = lax.ppermute(jnp.where(odd, last, first), "dom", both_ways[1])
    return inner, outer


def sorted_rims(inner, outer):
    odd = lax.axis_index("dom") % 2 == 1
    return jnp.where(odd, inner, outer), jnp.where(odd, outer, inner)


def joined(values):
    return list(lax.optimization_barrier(tuple(values)))


def gather_step(held, orders, step):
    return [swap(value, order[-1 - step]) for value, order in zip(held, orders)]


def both(held, arrived):
    return [jnp.concatenate(pair, axis=0) for pair in zip(held, arrived)]


def added(halves, arrived):
    totals = [kept.astype(F32) + value.astype(F32) for (kept, _), value in zip(halves, arrived)]
    cut = totals[0].shape[0] // 2
    return [(total[:cut], total[cut:].astype(BF16)) for total in totals]


def dot(a, b):
    return jnp.dot(a, b, preferred_element_type=F32)


def dot_t(a, b):
    return lax.dot_general(a, b, (((1,), (1,)), ((), ())), preferred_element_type=F32)


def t_dot(a, b):
    return lax.dot_general(a, b, (((0,), (0,)), ((), ())), preferred_element_type=F32)


def sigmoid(z):
    return 0.5 * jnp.tanh(0.5 * z) + 0.5


def normed(values):
    center = values - jnp.mean(values, axis=-1, keepdims=True)
    scale = lax.rsqrt(jnp.mean(center * center, axis=-1, keepdims=True) + norm_eps)
    return center * scale, scale


def norm_back(values, upstream):
    unit, scale = normed(values)
    first = jnp.mean(upstream, axis=-1, keepdims=True)
    second = jnp.mean(upstream * unit, axis=-1, keepdims=True)
    return scale * (upstream - first - unit * second)


def tiles(rows):
    return [slice(i, i + TILE) for i in range(0, rows, TILE)]


def silu_tiles(z_ref, a_ref):
    for t in tiles(z_ref.shape[0]):
        z = z_ref[t]
        a_ref[t] = (z * sigmoid(z)).astype(BF16)


def silu_and_slope(z):
    s = sigmoid(z)
    a = z * s
    return a.astype(BF16), s + a * (1.0 - s)


def one_hot(condition):
    return jnp.where(condition, 1.0, 0.0).astype(BF16)


def iota(shape, axis):
    return lax.broadcasted_iota(jnp.int32, shape, axis)


def repeat_matrix(rows):
    shape = (rows, rows // EPN)
    return one_hot((iota(shape, 0) >> 2) == iota(shape, 1))


def sum_matrix(rows):
    shape = (rows // EPN, rows)
    return one_hot((iota(shape, 1) >> 2) == iota(shape, 0))


def parts_of(first, second, groups):
    shares = first // groups, second // groups
    if all(share % 8 == 0 and share * groups == size for share, size in zip(shares, (first, second))):
        return [(0, shares[0]), (first, shares[1])]
    return [(0, -(-(first + second) // (groups * 16)) * 16)]


def chunk_rows(parts):
    return -(-sum(rows for _, rows in parts) // 16) * 16


def total_rows(parts, groups):
    return max(base + rows * groups for base, rows in parts)


def starts_of(parts, device):
    return [pl.multiple_of(base + device * rows, 8) for base, rows in parts]


def deal(total_ref, kept_ref, sent_ref, order, parts, me):
    half, width = kept_ref.shape[0], kept_ref.shape[2]
    rows = kept_ref.shape[1] // STREAMS
    spare = rows - sum(count for _, count in parts)
    for q, offset in enumerate(places(order)):
        starts = starts_of(parts, me ^ offset)
        for s in range(STREAMS):
            columns = slice(s * width, (s + 1) * width)
            values = [
                total_ref[pl.ds(start, count), columns] for start, (_, count) in zip(starts, parts)
            ]
            if spare:
                values.append(jnp.zeros((spare, width), F32))
            value = jnp.concatenate(values, axis=0) if len(values) > 1 else values[0]
            if q < half:
                kept_ref[q, s * rows : (s + 1) * rows] = value.astype(kept_ref.dtype)
            else:
                sent_ref[q - half, s * rows : (s + 1) * rows] = value.astype(BF16)


def edge_forward(src_ref, before_ref, node_ref, after_ref, edge_ref, w_in_ref, w_out_ref,
                 out_ref, sum_ref, z_ref, y_ref, ext_ref, x_ref, a_ref):
    step = pl.program_id(0)
    count, latent = node_ref.shape
    rows = edge_ref.shape[0]
    targets = rows // EPN

    @pl.when(step == 0)
    def _():
        ext_ref[:RIM] = before_ref[...]
        ext_ref[RIM : RIM + count] = node_ref[...]
        ext_ref[RIM + count :] = after_ref[...]

    hit = one_hot(iota((count + 2 * RIM, rows), 0) == src_ref[0])
    own = node_ref[pl.ds(pl.multiple_of(step * targets, targets), targets), :]
    x_ref[:, :latent] = edge_ref[...]
    x_ref[:, latent : 2 * latent] = t_dot(hit, ext_ref[...]).astype(BF16)
    x_ref[:, 2 * latent :] = dot(repeat_matrix(rows), own).astype(BF16)
    z_ref[...] = dot(x_ref[...], w_in_ref[...])
    silu_tiles(z_ref, a_ref)
    y_ref[...] = dot(a_ref[...], w_out_ref[...])
    for t in tiles(rows):
        out_ref[t] = (edge_ref[t].astype(F32) + normed(y_ref[t])[0]).astype(BF16)
    sum_ref[...] = dot(sum_matrix(rows), out_ref[...]).astype(BF16)


def edge_backward(orders, parts, me_ref, src_ref, before_ref, node_ref, after_ref, edge_ref, z_ref, y_ref,
                  cot_ref, mesh_ref, partial_ref, w_in_ref, w_out_ref,
                  grad_ref, h_ref, low_ref, high_ref, kept_ref, sent_ref,
                  ext_ref, by_source_ref, by_target_ref, total_ref):
    step = pl.program_id(0)
    count, latent = node_ref.shape
    rows = edge_ref.shape[0]
    targets = rows // EPN

    @pl.when(step == 0)
    def _():
        by_source_ref[...] = jnp.zeros_like(by_source_ref)
        total_ref[...] = jnp.zeros_like(total_ref)

    upstream = cot_ref[...].astype(F32) + dot(repeat_matrix(rows), mesh_ref[...])
    d_y = norm_back(y_ref[...], upstream).astype(BF16)
    a, slope = silu_and_slope(z_ref[...])
    total_ref[3 * latent : 4 * latent] += t_dot(a, d_y)
    d_z = (dot_t(d_y, w_out_ref[...]) * slope).astype(BF16)
    total_ref[:latent] += t_dot(edge_ref[...], d_z)
    grad_ref[...] = (upstream + dot_t(d_z, w_in_ref[:latent])).astype(BF16)
    hit = one_hot(iota((count + 2 * RIM, rows), 0) == src_ref[0])
    by_source_ref[...] += dot(hit, d_z)
    place = pl.ds(pl.multiple_of(step * targets, targets), targets)
    by_target_ref[place, :] = dot(sum_matrix(rows), d_z)

    @pl.when(step == pl.num_programs(0) - 1)
    def _():
        ext_ref[:RIM] = before_ref[...]
        ext_ref[RIM : RIM + count] = node_ref[...]
        ext_ref[RIM + count :] = after_ref[...]
        by_source = by_source_ref[...].astype(BF16)
        total_ref[latent : 2 * latent] = t_dot(ext_ref[...], by_source)
        back = dot_t(by_source, w_in_ref[latent : 2 * latent])
        low_ref[...] = back[:RIM].astype(BF16)
        high_ref[...] = back[RIM + count :].astype(BF16)
        by_target = by_target_ref[...].astype(BF16)
        total_ref[2 * latent : 3 * latent] = t_dot(node_ref[...], by_target)
        h_ref[...] = (
            partial_ref[...] + back[RIM : RIM + count] + dot_t(by_target, w_in_ref[2 * latent :])
        )
        deal(total_ref, kept_ref, sent_ref, orders[0], parts, me_ref[0])


def node_and_contact(orders, node_parts, contact_parts, row_count, me_ref, host_ref, remote_ref, block_ref, *refs):
    count = 2 * STREAMS * row_count
    far = refs[:count]
    (node_ref, mesh_ref, cot_ref, nw_in_ref, nw_out_ref, cw_in_ref, cw_out_ref,
     out_ref, h_ref, d_mesh_ref, nkept_ref, nsent_ref, ckept_ref, csent_ref,
     *slab_refs) = refs[count : count + 16]
    (x_ref, z_ref, y_ref, sum_ref, total_ref, x_node_ref, d_contact_ref, g_ref,
     nw_in, nw_out, nkept, nsent, sems) = refs[count + 16 :]
    loads = [
        pltpu.make_async_copy(nw_in_ref, nw_in, sems.at[0]),
        pltpu.make_async_copy(nw_out_ref, nw_out, sems.at[1]),
    ]
    stores = [
        pltpu.make_async_copy(nkept, nkept_ref, sems.at[2]),
        pltpu.make_async_copy(nsent, nsent_ref, sems.at[3]),
    ]
    for copy in loads:
        copy.start()
    latent = node_ref.shape[1]
    width = latent // STREAMS
    me = me_ref[0]
    chunk = min(4, row_count)
    blocks = node_ref.shape[0] // BLOCK
    half = nkept_ref.shape[0]

    def own_rows(row):
        return pl.ds(pl.multiple_of(block_ref[row] * BLOCK, BLOCK), BLOCK)

    sum_ref[...] = jnp.zeros_like(sum_ref)
    for row in range(row_count):
        rows = slice(row * BLOCK, (row + 1) * BLOCK)
        x_ref[rows, :latent] = node_ref[own_rows(row), :]
        for s, order in enumerate(orders):
            columns = slice(latent + s * width, latent + (s + 1) * width)
            near, away = far[2 * (row * STREAMS + s)], far[2 * (row * STREAMS + s) + 1]
            is_near = place_of(order, host_ref[row] ^ me) < half

            @pl.when(is_near)
            def _():
                x_ref[rows, columns] = near[0]

            @pl.when(jnp.logical_not(is_near))
            def _():
                x_ref[rows, columns] = away[0]
    for first in range(0, row_count, chunk):
        rows = slice(first * BLOCK, (first + chunk) * BLOCK)
        z = dot(x_ref[rows], cw_in_ref[...])
        y = dot(silu_and_slope(z)[0], cw_out_ref[...])
        z_ref[rows] = z
        y_ref[rows] = y
        message = normed(y)[0].astype(BF16).astype(F32)
        for row in range(first, first + chunk):
            part = message[(row - first) * BLOCK : (row - first + 1) * BLOCK]
            sum_ref[own_rows(row), :] += part

    for copy in loads:
        copy.wait()
    node = node_ref[...]
    x_node_ref[:, :latent] = node
    x_node_ref[:, latent : 2 * latent] = mesh_ref[...]
    x_node_ref[:, 2 * latent :] = sum_ref[...].astype(BF16)
    z = dot(x_node_ref[...], nw_in[...])
    a, slope = silu_and_slope(z)
    y = dot(a, nw_out[...])
    out_ref[...] = (node.astype(F32) + normed(y)[0]).astype(BF16)
    upstream = cot_ref[...].astype(F32)
    d_y = norm_back(y, upstream).astype(BF16)
    total_ref[3 * latent : 4 * latent] = t_dot(a, d_y)
    d_z = (dot_t(d_y, nw_out[...]) * slope).astype(BF16)
    total_ref[: 3 * latent] = t_dot(x_node_ref[...], d_z)
    if total_ref.shape[0] > 4 * latent:
        total_ref[4 * latent :] = jnp.zeros((total_ref.shape[0] - 4 * latent, latent), F32)
    d_x = dot_t(d_z, nw_in[...])
    h_ref[...] = upstream + d_x[:, :latent]
    d_mesh_ref[...] = d_x[:, latent : 2 * latent].astype(BF16)
    d_contact_ref[...] = d_x[:, 2 * latent :].astype(BF16).astype(F32)
    deal(total_ref, nkept, nsent, orders[1], node_parts, me)
    for copy in stores:
        copy.start()

    total_ref[: 3 * latent] = jnp.zeros((3 * latent, latent), F32)
    if total_ref.shape[0] > 3 * latent:
        total_ref[3 * latent :] = jnp.zeros((total_ref.shape[0] - 3 * latent, latent), F32)
    for first in range(0, row_count, chunk):
        rows = slice(first * BLOCK, (first + chunk) * BLOCK)
        for row in range(first, first + chunk):
            part = slice((row - first) * BLOCK, (row - first + 1) * BLOCK)
            g_ref[part, :latent] = d_contact_ref[own_rows(row), :]
        d_y = norm_back(y_ref[rows], g_ref[:, :latent]).astype(BF16)
        a, slope = silu_and_slope(z_ref[rows])
        total_ref[2 * latent : 3 * latent] += t_dot(a, d_y)
        d_z = (dot_t(d_y, cw_out_ref[...]) * slope).astype(BF16)
        total_ref[: 2 * latent] += t_dot(x_ref[rows], d_z)
        g_ref[...] = dot_t(d_z, cw_in_ref[...])
        for row in range(first, first + chunk):
            part = slice((row - first) * BLOCK, (row - first + 1) * BLOCK)
            h_ref[own_rows(row), :] += g_ref[part, :latent]
            cut = latent
            for ref in slab_refs:
                columns = ref.shape[2]
                ref[row] = g_ref[part, cut : cut + columns].astype(BF16)
                cut += columns
    deal(total_ref, ckept_ref, csent_ref, orders[2], contact_parts, me)
    for copy in stores:
        copy.wait()


def pick_blocks(orders, blocks, row_count, me_ref, *refs):
    named, quarters, outs, sems = refs[:3], refs[3:9], refs[9:12], refs[12]
    copies = []
    for s, order in enumerate(orders):
        near, away = quarters[2 * s], quarters[2 * s + 1]
        count = near.shape[0]
        for i in range(row_count):
            spot = place_of(order, named[s][i] ^ me_ref[0]) * blocks + named[s][row_count + i]
            spot = jnp.where(spot < 2 * count, spot, 0)
            is_near = spot < count
            sem = sems.at[len(copies)]

            @pl.when(is_near)
            def _():
                pltpu.make_async_copy(near.at[spot], outs[s].at[i], sem).start()

            @pl.when(jnp.logical_not(is_near))
            def _():
                pltpu.make_async_copy(away.at[spot - count], outs[s].at[i], sem).start()

            copies.append(pltpu.make_async_copy(near.at[0], outs[s].at[i], sem))
    for copy in copies:
        copy.wait()


def add_to_places(orders, blocks, me_ref, host_ref, remote_ref, *refs):
    named, own, arrived, outs = refs[:2], refs[2:4], refs[4:6], refs[6:]
    row_count = own[0].shape[0]
    width = outs[0].shape[2]
    views = [(0, slice(0, width)), (0, slice(width, 2 * width)), (1, slice(0, width))]
    me = me_ref[0]
    for out in outs:
        out[...] = jnp.zeros_like(out)
    for s, order in enumerate(orders):
        array, columns = views[s]

        def place(source, i, host, remote):
            spot = place_of(order, host ^ me) * blocks + remote
            for half in range(2):
                out = outs[half * STREAMS + s]
                slots = out.shape[0]
                here = spot - half * slots

                @pl.when(jnp.logical_and(here >= 0, here < slots))
                def _():
                    total = out[here].astype(F32) + source[array][i, :, columns].astype(F32)
                    out[here] = total.astype(out.dtype)

        for i in range(row_count):
            place(own, i, host_ref[i], remote_ref[i])
            place(arrived, i, named[array][i], named[array][row_count + i])


def unpack(orders, parts, half_index, me_ref, *refs):
    halves, rest = refs[:STREAMS], refs[STREAMS:]
    outs, rows_refs, sems = rest[-3 * STREAMS - 1 : -STREAMS - 1], rest[-STREAMS - 1 : -1], rest[-1]
    copies = []
    for s, order in enumerate(orders):
        count, width = halves[s].shape[0], halves[s].shape[2]
        rows = halves[s].shape[1] // STREAMS
        for q in range(count):
            for c in range(STREAMS):
                value = halves[s][q, c * rows : (c + 1) * rows].astype(F32)
                rows_refs[s][q, :, c * width : (c + 1) * width] = value
            device = me_ref[0] ^ places(order)[half_index * count + q]
            done = 0
            for p, (_, share) in enumerate(parts[s]):
                start = pl.multiple_of(device * share, 8)
                copy = pltpu.make_async_copy(
                    rows_refs[s].at[q, pl.ds(done, share)],
                    outs[2 * s + p].at[pl.ds(start, share)],
                    sems.at[len(copies)],
                )
                copy.start()
                copies.append(copy)
                done += share
    for copy in copies:
        copy.wait()


def unpack_whole(order, me_ref, near_ref, far_ref, first_ref, second_ref, total_ref):
    half, width = near_ref.shape[0], near_ref.shape[2]
    rows = near_ref.shape[1] // STREAMS
    for q, offset in enumerate(places(order)):
        ref, place = (near_ref, q) if q < half else (far_ref, q - half)
        start = pl.multiple_of((me_ref[0] ^ offset) * rows, 8)
        for s in range(STREAMS):
            value = ref[place, s * rows : (s + 1) * rows].astype(F32)
            total_ref[pl.ds(start, rows), s * width : (s + 1) * width] = value
    cut = first_ref.shape[0]
    first_ref[...] = total_ref[:cut]
    second_ref[...] = total_ref[cut : cut + second_ref.shape[0]]


def params(axes=0):
    return pltpu.CompilerParams(
        vmem_limit_bytes=VMEM_LIMIT,
        dimension_semantics=("arbitrary",) * axes if axes else None,
    )


def cost(flops, moved):
    return pl.CostEstimate(flops=flops, bytes_accessed=moved, transcendentals=0)


def whole(array_shape):
    return pl.BlockSpec(array_shape, lambda *_: (0,) * len(array_shape))


def struct(shape, dtype):
    return jax.ShapeDtypeStruct(shape, dtype)


def on_device(
    node_state,
    edge_state,
    edge_source,
    contact_block,
    contact_host,
    contact_remote,
    w_edge_in,
    w_edge_out,
    w_node_in,
    w_node_out,
    w_contact_in,
    w_contact_out,
    node_cot,
    edge_cot,
):
    node_count, latent = node_state.shape
    edge_count = edge_state.shape[0]
    groups = lax.axis_size("dom")
    blocks = node_count // BLOCK
    row_count = contact_block.shape[0]
    width = latent // STREAMS
    orders = exchange_orders(groups)
    me = lax.axis_index("dom").astype(jnp.int32).reshape(1)
    host = contact_host[:, 0]
    smem = pl.BlockSpec(memory_space=pltpu.SMEM)
    anywhere = pl.BlockSpec(memory_space=pl.ANY)

    inner, outer = swap_rims(node_state[:RIM], node_state[node_count - RIM :])
    last = len(orders[0]) - 1
    far_bit = orders[0][-1]
    half = groups // 2
    rows_named = jnp.concatenate([host, contact_remote])
    arrived, inner, outer, *named = joined(
        [swap(node_state, far_bit), inner, outer]
        + [swap(rows_named, order[0]) for order in orders[:2]]
    )
    before, after = sorted_rims(inner, outer)
    pair = jnp.stack([node_state, arrived])
    slabs = [pair[:, :, s * width : (s + 1) * width] for s in range(STREAMS)]
    for step in range(1, last):
        if step == last - 1:
            *slabs, before, rows_named = joined([*slabs, before, rows_named])
            named.append(swap(rows_named, orders[2][0]))
        arrived = gather_step(slabs, orders, step)
        if step < last - 1:
            slabs = both(slabs, joined(arrived))

    steps = edge_count // EDGE_ROWS
    sources = edge_source.reshape(steps, 1, EDGE_ROWS)
    edge_block = pl.BlockSpec((EDGE_ROWS, latent), lambda i: (i, 0))
    node_block = pl.BlockSpec((EDGE_ROWS // EPN, latent), lambda i: (i, 0))
    source_block = pl.BlockSpec((1, 1, EDGE_ROWS), lambda i: (i, 0, 0))
    rim_block = whole((RIM, latent))
    extended_rows = node_count + 2 * RIM
    edge_out, mesh_sum, e_pre, e_linear = pl.pallas_call(
        edge_forward,
        grid=(steps,),
        in_specs=[
            source_block,
            rim_block,
            whole(node_state.shape),
            rim_block,
            edge_block,
            whole(w_edge_in.shape),
            whole(w_edge_out.shape),
        ],
        out_specs=[edge_block, node_block, edge_block, edge_block],
        out_shape=[
            struct((edge_count, latent), BF16),
            struct((node_count, latent), BF16),
            struct((edge_count, latent), F32),
            struct((edge_count, latent), F32),
        ],
        scratch_shapes=[
            pltpu.VMEM((extended_rows, latent), BF16),
            pltpu.VMEM((EDGE_ROWS, 3 * latent), BF16),
            pltpu.VMEM((EDGE_ROWS, latent), BF16),
        ],
        compiler_params=params(1),
        cost_estimate=cost(2 * edge_count * latent * latent * 6, edge_count * latent * 16),
        name="edge_forward",
    )(sources, before, node_state, after, edge_state, w_edge_in, w_edge_out)

    *arrived, named[2], mesh_sum = joined([*arrived, named[2], mesh_sum])
    quarters = [
        value.reshape(half * blocks // 2, BLOCK, width)
        for pair in zip(slabs, arrived)
        for value in pair
    ]
    picked = pl.pallas_call(
        functools.partial(pick_blocks, orders, blocks, row_count),
        in_specs=[smem] * (1 + STREAMS) + [anywhere] * (2 * STREAMS),
        out_specs=[anywhere] * STREAMS,
        out_shape=[struct((row_count, BLOCK, width), BF16)] * STREAMS,
        scratch_shapes=[pltpu.SemaphoreType.DMA((STREAMS * row_count,))],
        compiler_params=params(),
        cost_estimate=cost(0, 2**20),
        name="pick_blocks",
    )(me, *named, *quarters)
    joined_now = joined([*picked, *quarters])
    picked, quarters = joined_now[:STREAMS], joined_now[STREAMS:]
    slabs = [jnp.concatenate(quarters[2 * s : 2 * s + 2], axis=0) for s in range(STREAMS)]
    answered = [swap(value, order[0]) for value, order in zip(picked, orders)]

    def near_spec(row, s):
        def index(i, me_ref, host_ref, remote_ref, block_ref):
            spot = place_of(orders[s], host_ref[row] ^ me_ref[0])
            return (jnp.where(spot < half, spot * blocks + remote_ref[row], 0), 0, 0)

        return pl.BlockSpec((1, BLOCK, width), index)

    def answer_spec(row):
        return pl.BlockSpec((1, BLOCK, width), lambda *_: (row, 0, 0))

    far = []
    for row in range(row_count):
        for s in range(STREAMS):
            far += [(near_spec(row, s), slabs[s]), (answer_spec(row), answered[s])]
    far_specs, far_args = [spec for spec, _ in far], [arg for _, arg in far]
    matrices = [(w_edge_in, w_edge_out), (w_node_in, w_node_out), (w_contact_in, w_contact_out)]
    parts = [parts_of(first.shape[0], second.shape[0], groups) for first, second in matrices]
    pair_rows = [chunk_rows(part) for part in parts]
    halves = lambda rows: [struct((half, rows * STREAMS, width), BF16)] * 2
    remote_parts = [
        struct((row_count, BLOCK, columns), BF16) for columns in (2 * width, latent - 2 * width)
    ]
    b_out = [
        struct((node_count, latent), BF16),
        struct((node_count, latent), F32),
        struct((node_count, latent), BF16),
        *halves(pair_rows[1]),
        *halves(pair_rows[2]),
        *remote_parts,
    ]
    b_args = [node_state, mesh_sum, node_cot, w_node_in, w_node_out, w_contact_in, w_contact_out]
    contact_rows = row_count * BLOCK
    chunk_length = min(4, row_count) * BLOCK
    (node_out, partial_h, d_mesh, n_kept, n_sent, c_kept, c_sent, *away) = pl.pallas_call(
        functools.partial(node_and_contact, orders, parts[1], parts[2], row_count),
        grid_spec=pltpu.PrefetchScalarGridSpec(
            num_scalar_prefetch=4,
            grid=(1,),
            in_specs=far_specs
            + [anywhere if 3 <= i <= 4 else whole(arg.shape) for i, arg in enumerate(b_args)],
            out_specs=[
                anywhere if 3 <= i <= 4 else whole(out.shape) for i, out in enumerate(b_out)
            ],
            scratch_shapes=[
                pltpu.VMEM((contact_rows, 2 * latent), BF16),
                pltpu.VMEM((contact_rows, latent), F32),
                pltpu.VMEM((contact_rows, latent), F32),
                pltpu.VMEM((node_count, latent), F32),
                pltpu.VMEM((max(total_rows(part, groups) for part in parts[1:]), latent), F32),
                pltpu.VMEM((node_count, 3 * latent), BF16),
                pltpu.VMEM((node_count, latent), F32),
                pltpu.VMEM((chunk_length, 2 * latent), F32),
                pltpu.VMEM(w_node_in.shape, BF16),
                pltpu.VMEM(w_node_out.shape, BF16),
                pltpu.VMEM(b_out[3].shape, BF16),
                pltpu.VMEM(b_out[4].shape, BF16),
                pltpu.SemaphoreType.DMA((4,)),
            ],
        ),
        out_shape=b_out,
        compiler_params=params(1),
        cost_estimate=cost(2 * (contact_rows * 9 + node_count * 12) * latent * latent, 12 * 2**20),
        name="node_and_contact",
    )(me, host, contact_remote, contact_block, *far_args, *b_args)

    back = return_orders(orders)
    away_arrived = [swap(value, order[0]) for value, order in zip(away, back[1:])]
    n_arrived, c_arrived = swap(n_sent, orders[1][0]), swap(c_sent, orders[2][0])

    edge_grad, near_h, low, high, e_kept, e_sent = pl.pallas_call(
        functools.partial(edge_backward, orders, parts[0]),
        grid=(steps,),
        in_specs=[
            smem,
            source_block,
            rim_block,
            whole(node_state.shape),
            rim_block,
            edge_block,
            edge_block,
            edge_block,
            edge_block,
            node_block,
            whole((node_count, latent)),
            whole(w_edge_in.shape),
            whole(w_edge_out.shape),
        ],
        out_specs=[
            edge_block,
            whole((node_count, latent)),
            rim_block,
            rim_block,
            *[whole((half, pair_rows[0] * STREAMS, width))] * 2,
        ],
        out_shape=[
            struct((edge_count, latent), BF16),
            struct((node_count, latent), F32),
            struct((RIM, latent), BF16),
            struct((RIM, latent), BF16),
            *halves(pair_rows[0]),
        ],
        scratch_shapes=[
            pltpu.VMEM((extended_rows, latent), BF16),
            pltpu.VMEM((extended_rows, latent), F32),
            pltpu.VMEM((node_count, latent), F32),
            pltpu.VMEM((total_rows(parts[0], groups), latent), F32),
        ],
        compiler_params=params(1),
        cost_estimate=cost(2 * edge_count * latent * latent * 8, edge_count * latent * 20),
        name="edge_backward",
    )(me, sources, before, node_state, after, edge_state, e_pre, e_linear, edge_cot, d_mesh,
      partial_h, w_edge_in, w_edge_out)

    *away_arrived, e_sent = joined([*away_arrived, e_sent])
    e_arrived = swap(e_sent, orders[0][0])
    slots = half * blocks // 2
    placed = pl.pallas_call(
        functools.partial(add_to_places, back, blocks),
        in_specs=[smem] * 5 + [pl.BlockSpec(memory_space=pltpu.VMEM)] * 4,
        out_specs=[pl.BlockSpec(memory_space=pltpu.VMEM)] * (2 * STREAMS),
        out_shape=[
            struct((slots, BLOCK, width), dtype) for dtype in (F32, BF16) for _ in range(STREAMS)
        ],
        compiler_params=params(),
        cost_estimate=cost(0, 6 * 2**20),
        name="add_to_places",
    )(me, host, contact_remote, *named[:2], *away, *away_arrived)
    away_kept = placed[:STREAMS]
    n_arrived, c_arrived, *away_sent = joined([n_arrived, c_arrived, *placed[STREAMS:]])
    arrived = [swap(sent, order[1]) for sent, order in zip(away_sent, back)]
    *arrived, e_arrived = joined([*arrived, e_arrived])
    away = list(zip(away_kept, away_sent))
    away = added(away, arrived)
    weights = added(
        [(e_kept, e_sent), (n_kept, n_sent), (c_kept, c_sent)], [e_arrived, n_arrived, c_arrived]
    )
    for step in range(1, last - 1):
        sent = [jnp.concatenate([a[1], w[1]], axis=1) for a, w in zip(away, weights)]
        arrived = joined([swap(value, order[step]) for value, order in zip(sent, orders)])
        away = added(away, [value[:, :BLOCK] for value in arrived])
        weights = added(weights, [value[:, BLOCK:] for value in arrived])
    arrived = joined([swap(w[1], order[last - 1]) for w, order in zip(weights, orders)])
    mine = jnp.concatenate(
        [(w[0] + value.astype(F32)).astype(BF16) for w, value in zip(weights, arrived)], axis=1
    )
    mine, low, high = joined([mine, low, high])
    theirs, *rims = joined([swap(mine, far_bit), *swap_rims(low, high)])
    high, low = sorted_rims(*rims)
    pair = (mine.astype(F32) + theirs[::-1].astype(F32)).astype(BF16)
    cuts = [sum(pair_rows[:s]) * STREAMS for s in range(STREAMS + 1)]
    sums = [pair[:, cuts[s] : cuts[s + 1]] for s in range(STREAMS)]
    for step in range(1, last):
        sums = both(sums, joined(gather_step(sums, orders, step)))
    away_sent = jnp.concatenate([sent for _, sent in away], axis=2)
    *sums, away_sent = joined([*sums, away_sent])
    gathered = list(zip(sums, gather_step(sums, orders, last)))
    returned = swap(away_sent, far_bit)
    kept = jnp.concatenate([kept for kept, _ in away], axis=2)
    returned = (kept + returned.astype(F32)).reshape(node_count, latent)
    vmem = pl.BlockSpec(memory_space=pltpu.VMEM)
    if all(len(part) == 2 for part in parts):
        summed = []
        for side in range(2):
            summed = pl.pallas_call(
                functools.partial(unpack, orders, parts, side),
                in_specs=[smem] + [vmem] * STREAMS + [anywhere] * len(summed),
                out_specs=[anywhere] * (2 * STREAMS),
                out_shape=[struct(w.shape, F32) for pair in matrices for w in pair],
                scratch_shapes=[
                    *[pltpu.VMEM((half, rows, latent), F32) for rows in pair_rows],
                    pltpu.SemaphoreType.DMA((2 * STREAMS * half,)),
                ],
                input_output_aliases={1 + STREAMS + i: i for i in range(len(summed))},
                compiler_params=params(),
                cost_estimate=cost(0, half * sum(pair_rows) * latent * 10),
                name="unpack",
            )(me, *[pair[side] for pair in gathered], *summed)
    else:
        summed = []
        for s, (first, second) in enumerate(matrices):
            summed += pl.pallas_call(
                functools.partial(unpack_whole, orders[s]),
                in_specs=[smem] + [vmem] * 2,
                out_specs=[vmem] * 2,
                out_shape=[struct(first.shape, F32), struct(second.shape, F32)],
                scratch_shapes=[pltpu.VMEM((pair_rows[s] * groups, latent), F32)],
                compiler_params=params(),
                name="unpack_whole",
            )(me, *gathered[s])

    rims = jnp.concatenate(
        [
            high.astype(F32),
            jnp.zeros((node_count - 2 * RIM, latent), F32),
            low.astype(F32),
        ],
        axis=0,
    )
    node_grad = (near_h + rims + returned).astype(BF16)
    return (node_out, edge_out, node_grad, edge_grad, *summed)


def solution(mesh):
    rows = P(("rep", "dom"), None)
    flat = P(("rep", "dom"))
    weight = P("rep", None)
    in_specs = (rows, rows, flat, flat, rows, flat) + (weight,) * 6 + (rows, rows)
    out_specs = (rows,) * 4 + (weight,) * 6
    return jax.shard_map(
        on_device, mesh=mesh, in_specs=in_specs, out_specs=out_specs, check_vma=False
    )
```

```python
import functools

import jax
import jax.numpy as jnp
from jax import lax
from jax.experimental import pallas as pl
from jax.experimental.pallas import tpu as pltpu
from jax.sharding import PartitionSpec as P

BLOCK = 128
EPN = 4
RIM = 64
EDGE_ROWS = 512
TILE = 32
STREAMS = 3
VMEM_LIMIT = 50 * 2**20
BF16 = jnp.bfloat16
F32 = jnp.float32


norm_eps = 1e-05


def exchange_orders(groups):
    bits = groups.bit_length() - 1
    low = list(range(bits - 1))
    turns = [r % max(1, len(low)) for r in range(STREAMS)]
    return [low[r:] + low[:r] + [bits - 1] for r in turns]


def return_orders(orders):
    heads = [(o[0], o[-2]) if s == 0 else (o[-2], o[0]) for s, o in enumerate(orders)]
    return [[*head, *o[1:-2], o[-1]] for head, o in zip(heads, orders)]


def places(order):
    bits = len(order)
    return [
        sum(((q >> (bits - 1 - i)) & 1) << b for i, b in enumerate(order)) for q in range(1 << bits)
    ]


def place_of(order, offset):
    bits = len(order)
    return sum(((offset >> b) & 1) << (bits - 1 - i) for i, b in enumerate(order))


def swap(value, bit):
    peers = lax.axis_size("dom")
    return lax.ppermute(value, "dom", [(i, i ^ (1 << bit)) for i in range(peers)])


def swap_rims(first, last):
    peers = lax.axis_size("dom")
    odd = lax.axis_index("dom") % 2 == 1
    pairs = [[(i, i + 1) for i in range(start, peers - 1, 2)] for start in range(2)]
    both_ways = [pair + [(j, i) for i, j in pair] for pair in pairs]
    inner = lax.ppermute(jnp.where(odd, first, last), "dom", both_ways[0])
    outer = lax.ppermute(jnp.where(odd, last, first), "dom", both_ways[1])
    return inner, outer


def sorted_rims(inner, outer):
    odd = lax.axis_index("dom") % 2 == 1
    return jnp.where(odd, inner, outer), jnp.where(odd, outer, inner)


def joined(values):
    return list(lax.optimization_barrier(tuple(values)))


def gather_step(held, orders, step):
    return [swap(value, order[-1 - step]) for value, order in zip(held, orders)]


def both(held, arrived):
    return [jnp.concatenate(pair, axis=0) for pair in zip(held, arrived)]


def added(halves, arrived):
    totals = [kept.astype(F32) + value.astype(F32) for (kept, _), value in zip(halves, arrived)]
    cut = totals[0].shape[0] // 2
    return [(total[:cut], total[cut:].astype(BF16)) for total in totals]


def dot(a, b):
    return jnp.dot(a, b, preferred_element_type=F32)


def dot_t(a, b):
    return lax.dot_general(a, b, (((1,), (1,)), ((), ())), preferred_element_type=F32)


def t_dot(a, b):
    return lax.dot_general(a, b, (((0,), (0,)), ((), ())), preferred_element_type=F32)


def sigmoid(z):
    return 0.5 * jnp.tanh(0.5 * z) + 0.5


def normed(values):
    center = values - jnp.mean(values, axis=-1, keepdims=True)
    scale = lax.rsqrt(jnp.mean(center * center, axis=-1, keepdims=True) + norm_eps)
    return center * scale, scale


def norm_back(values, upstream):
    unit, scale = normed(values)
    first = jnp.mean(upstream, axis=-1, keepdims=True)
    second = jnp.mean(upstream * unit, axis=-1, keepdims=True)
    return scale * (upstream - first - unit * second)


def tiles(rows):
    return [slice(i, i + TILE) for i in range(0, rows, TILE)]


def silu_tiles(z_ref, a_ref):
    for t in tiles(z_ref.shape[0]):
        z = z_ref[t]
        a_ref[t] = (z * sigmoid(z)).astype(BF16)


def silu_and_slope(z):
    s = sigmoid(z)
    a = z * s
    return a.astype(BF16), s + a * (1.0 - s)


def one_hot(condition):
    return jnp.where(condition, 1.0, 0.0).astype(BF16)


def iota(shape, axis):
    return lax.broadcasted_iota(jnp.int32, shape, axis)


def repeat_matrix(rows):
    shape = (rows, rows // EPN)
    return one_hot((iota(shape, 0) >> 2) == iota(shape, 1))


def sum_matrix(rows):
    shape = (rows // EPN, rows)
    return one_hot((iota(shape, 1) >> 2) == iota(shape, 0))


def parts_of(first, second, groups):
    shares = first // groups, second // groups
    if all(share % 8 == 0 and share * groups == size for share, size in zip(shares, (first, second))):
        return [(0, shares[0]), (first, shares[1])]
    return [(0, -(-(first + second) // (groups * 16)) * 16)]


def chunk_rows(parts):
    return -(-sum(rows for _, rows in parts) // 16) * 16


def total_rows(parts, groups):
    return max(base + rows * groups for base, rows in parts)


def starts_of(parts, device):
    return [pl.multiple_of(base + device * rows, 8) for base, rows in parts]


def deal(total_ref, kept_ref, sent_ref, order, parts, me):
    half, width = kept_ref.shape[0], kept_ref.shape[2]
    rows = kept_ref.shape[1] // STREAMS
    spare = rows - sum(count for _, count in parts)
    for q, offset in enumerate(places(order)):
        starts = starts_of(parts, me ^ offset)
        for s in range(STREAMS):
            columns = slice(s * width, (s + 1) * width)
            values = [
                total_ref[pl.ds(start, count), columns] for start, (_, count) in zip(starts, parts)
            ]
            if spare:
                values.append(jnp.zeros((spare, width), F32))
            value = jnp.concatenate(values, axis=0) if len(values) > 1 else values[0]
            if q < half:
                kept_ref[q, s * rows : (s + 1) * rows] = value.astype(kept_ref.dtype)
            else:
                sent_ref[q - half, s * rows : (s + 1) * rows] = value.astype(BF16)


def edge_forward(src_ref, before_ref, node_ref, after_ref, edge_ref, w_in_ref, w_out_ref,
                 out_ref, sum_ref, z_ref, y_ref, ext_ref, x_ref, a_ref):
    step = pl.program_id(0)
    count, latent = node_ref.shape
    rows = edge_ref.shape[0]
    targets = rows // EPN

    @pl.when(step == 0)
    def _():
        ext_ref[:RIM] = before_ref[...]
        ext_ref[RIM : RIM + count] = node_ref[...]
        ext_ref[RIM + count :] = after_ref[...]

    hit = one_hot(iota((count + 2 * RIM, rows), 0) == src_ref[0])
    own = node_ref[pl.ds(pl.multiple_of(step * targets, targets), targets), :]
    x_ref[:, :latent] = edge_ref[...]
    x_ref[:, latent : 2 * latent] = t_dot(hit, ext_ref[...]).astype(BF16)
    x_ref[:, 2 * latent :] = dot(repeat_matrix(rows), own).astype(BF16)
    z_ref[...] = dot(x_ref[...], w_in_ref[...])
    silu_tiles(z_ref, a_ref)
    y_ref[...] = dot(a_ref[...], w_out_ref[...])
    for t in tiles(rows):
        out_ref[t] = (edge_ref[t].astype(F32) + normed(y_ref[t])[0]).astype(BF16)
    sum_ref[...] = dot(sum_matrix(rows), out_ref[...]).astype(BF16)


def edge_backward(orders, parts, me_ref, src_ref, before_ref, node_ref, after_ref, edge_ref, z_ref, y_ref,
                  cot_ref, mesh_ref, partial_ref, w_in_ref, w_out_ref,
                  grad_ref, h_ref, low_ref, high_ref, kept_ref, sent_ref,
                  ext_ref, by_source_ref, by_target_ref, total_ref):
    step = pl.program_id(0)
    count, latent = node_ref.shape
    rows = edge_ref.shape[0]
    targets = rows // EPN

    @pl.when(step == 0)
    def _():
        by_source_ref[...] = jnp.zeros_like(by_source_ref)
        total_ref[...] = jnp.zeros_like(total_ref)

    upstream = cot_ref[...].astype(F32) + dot(repeat_matrix(rows), mesh_ref[...])
    d_y = norm_back(y_ref[...], upstream).astype(BF16)
    a, slope = silu_and_slope(z_ref[...])
    total_ref[3 * latent : 4 * latent] += t_dot(a, d_y)
    d_z = (dot_t(d_y, w_out_ref[...]) * slope).astype(BF16)
    total_ref[:latent] += t_dot(edge_ref[...], d_z)
    grad_ref[...] = (upstream + dot_t(d_z, w_in_ref[:latent])).astype(BF16)
    hit = one_hot(iota((count + 2 * RIM, rows), 0) == src_ref[0])
    by_source_ref[...] += dot(hit, d_z)
    place = pl.ds(pl.multiple_of(step * targets, targets), targets)
    by_target_ref[place, :] = dot(sum_matrix(rows), d_z)

    @pl.when(step == pl.num_programs(0) - 1)
    def _():
        ext_ref[:RIM] = before_ref[...]
        ext_ref[RIM : RIM + count] = node_ref[...]
        ext_ref[RIM + count :] = after_ref[...]
        by_source = by_source_ref[...].astype(BF16)
        total_ref[latent : 2 * latent] = t_dot(ext_ref[...], by_source)
        back = dot_t(by_source, w_in_ref[latent : 2 * latent])
        low_ref[...] = back[:RIM].astype(BF16)
        high_ref[...] = back[RIM + count :].astype(BF16)
        by_target = by_target_ref[...].astype(BF16)
        total_ref[2 * latent : 3 * latent] = t_dot(node_ref[...], by_target)
        h_ref[...] = (
            partial_ref[...] + back[RIM : RIM + count] + dot_t(by_target, w_in_ref[2 * latent :])
        )
        deal(total_ref, kept_ref, sent_ref, orders[0], parts, me_ref[0])


def node_and_contact(orders, node_parts, contact_parts, row_count, me_ref, host_ref, remote_ref, block_ref, *refs):
    count = 2 * STREAMS * row_count
    far = refs[:count]
    (node_ref, mesh_ref, cot_ref, nw_in_ref, nw_out_ref, cw_in_ref, cw_out_ref,
     out_ref, h_ref, d_mesh_ref, nkept_ref, nsent_ref, ckept_ref, csent_ref,
     *slab_refs) = refs[count : count + 16]
    (x_ref, z_ref, y_ref, sum_ref, total_ref, x_node_ref, d_contact_ref, g_ref,
     nw_in, nw_out, nkept, nsent, sems) = refs[count + 16 :]
    loads = [
        pltpu.make_async_copy(nw_in_ref, nw_in, sems.at[0]),
        pltpu.make_async_copy(nw_out_ref, nw_out, sems.at[1]),
    ]
    stores = [
        pltpu.make_async_copy(nkept, nkept_ref, sems.at[2]),
        pltpu.make_async_copy(nsent, nsent_ref, sems.at[3]),
    ]
    for copy in loads:
        copy.start()
    latent = node_ref.shape[1]
    width = latent // STREAMS
    me = me_ref[0]
    chunk = min(4, row_count)
    blocks = node_ref.shape[0] // BLOCK
    half = nkept_ref.shape[0]

    def own_rows(row):
        return pl.ds(pl.multiple_of(block_ref[row] * BLOCK, BLOCK), BLOCK)

    sum_ref[...] = jnp.zeros_like(sum_ref)
    for row in range(row_count):
        rows = slice(row * BLOCK, (row + 1) * BLOCK)
        x_ref[rows, :latent] = node_ref[own_rows(row), :]
        for s, order in enumerate(orders):
            columns = slice(latent + s * width, latent + (s + 1) * width)
            near, away = far[2 * (row * STREAMS + s)], far[2 * (row * STREAMS + s) + 1]
            is_near = place_of(order, host_ref[row] ^ me) < half

            @pl.when(is_near)
            def _():
                x_ref[rows, columns] = near[0]

            @pl.when(jnp.logical_not(is_near))
            def _():
                x_ref[rows, columns] = away[0]
    for first in range(0, row_count, chunk):
        rows = slice(first * BLOCK, (first + chunk) * BLOCK)
        z = dot(x_ref[rows], cw_in_ref[...])
        y = dot(silu_and_slope(z)[0], cw_out_ref[...])
        z_ref[rows] = z
        y_ref[rows] = y
        message = normed(y)[0].astype(BF16).astype(F32)
        for row in range(first, first + chunk):
            part = message[(row - first) * BLOCK : (row - first + 1) * BLOCK]
            sum_ref[own_rows(row), :] += part

    for copy in loads:
        copy.wait()
    node = node_ref[...]
    x_node_ref[:, :latent] = node
    x_node_ref[:, latent : 2 * latent] = mesh_ref[...]
    x_node_ref[:, 2 * latent :] = sum_ref[...].astype(BF16)
    z = dot(x_node_ref[...], nw_in[...])
    a, slope = silu_and_slope(z)
    y = dot(a, nw_out[...])
    out_ref[...] = (node.astype(F32) + normed(y)[0]).astype(BF16)
    upstream = cot_ref[...].astype(F32)
    d_y = norm_back(y, upstream).astype(BF16)
    total_ref[3 * latent : 4 * latent] = t_dot(a, d_y)
    d_z = (dot_t(d_y, nw_out[...]) * slope).astype(BF16)
    total_ref[: 3 * latent] = t_dot(x_node_ref[...], d_z)
    if total_ref.shape[0] > 4 * latent:
        total_ref[4 * latent :] = jnp.zeros((total_ref.shape[0] - 4 * latent, latent), F32)
    d_x = dot_t(d_z, nw_in[...])
    h_ref[...] = upstream + d_x[:, :latent]
    d_mesh_ref[...] = d_x[:, latent : 2 * latent].astype(BF16)
    d_contact_ref[...] = d_x[:, 2 * latent :].astype(BF16).astype(F32)
    deal(total_ref, nkept, nsent, orders[1], node_parts, me)
    for copy in stores:
        copy.start()

    total_ref[: 3 * latent] = jnp.zeros((3 * latent, latent), F32)
    if total_ref.shape[0] > 3 * latent:
        total_ref[3 * latent :] = jnp.zeros((total_ref.shape[0] - 3 * latent, latent), F32)
    for first in range(0, row_count, chunk):
        rows = slice(first * BLOCK, (first + chunk) * BLOCK)
        for row in range(first, first + chunk):
            part = slice((row - first) * BLOCK, (row - first + 1) * BLOCK)
            g_ref[part, :latent] = d_contact_ref[own_rows(row), :]
        d_y = norm_back(y_ref[rows], g_ref[:, :latent]).astype(BF16)
        a, slope = silu_and_slope(z_ref[rows])
        total_ref[2 * latent : 3 * latent] += t_dot(a, d_y)
        d_z = (dot_t(d_y, cw_out_ref[...]) * slope).astype(BF16)
        total_ref[: 2 * latent] += t_dot(x_ref[rows], d_z)
        g_ref[...] = dot_t(d_z, cw_in_ref[...])
        for row in range(first, first + chunk):
            part = slice((row - first) * BLOCK, (row - first + 1) * BLOCK)
            h_ref[own_rows(row), :] += g_ref[part, :latent]
            cut = latent
            for ref in slab_refs:
                columns = ref.shape[2]
                ref[row] = g_ref[part, cut : cut + columns].astype(BF16)
                cut += columns
    deal(total_ref, ckept_ref, csent_ref, orders[2], contact_parts, me)
    for copy in stores:
        copy.wait()


def pick_blocks(orders, blocks, row_count, me_ref, *refs):
    named, quarters, outs, sems = refs[:3], refs[3:9], refs[9:12], refs[12]
    copies = []
    for s, order in enumerate(orders):
        near, away = quarters[2 * s], quarters[2 * s + 1]
        count = near.shape[0]
        for i in range(row_count):
            spot = place_of(order, named[s][i] ^ me_ref[0]) * blocks + named[s][row_count + i]
            spot = jnp.where(spot < 2 * count, spot, 0)
            is_near = spot < count
            sem = sems.at[len(copies)]

            @pl.when(is_near)
            def _():
                pltpu.make_async_copy(near.at[spot], outs[s].at[i], sem).start()

            @pl.when(jnp.logical_not(is_near))
            def _():
                pltpu.make_async_copy(away.at[spot - count], outs[s].at[i], sem).start()

            copies.append(pltpu.make_async_copy(near.at[0], outs[s].at[i], sem))
    for copy in copies:
        copy.wait()


def add_to_places(orders, blocks, me_ref, host_ref, remote_ref, *refs):
    named, own, arrived, outs = refs[:2], refs[2:4], refs[4:6], refs[6:]
    row_count = own[0].shape[0]
    width = outs[0].shape[2]
    views = [(0, slice(0, width)), (0, slice(width, 2 * width)), (1, slice(0, width))]
    me = me_ref[0]
    for out in outs:
        out[...] = jnp.zeros_like(out)
    for s, order in enumerate(orders):
        array, columns = views[s]

        def place(source, i, host, remote):
            spot = place_of(order, host ^ me) * blocks + remote
            for half in range(2):
                out = outs[half * STREAMS + s]
                slots = out.shape[0]
                here = spot - half * slots

                @pl.when(jnp.logical_and(here >= 0, here < slots))
                def _():
                    total = out[here].astype(F32) + source[array][i, :, columns].astype(F32)
                    out[here] = total.astype(out.dtype)

        for i in range(row_count):
            place(own, i, host_ref[i], remote_ref[i])
            place(arrived, i, named[array][i], named[array][row_count + i])


def unpack(orders, parts, half_index, me_ref, *refs):
    halves, rest = refs[:STREAMS], refs[STREAMS:]
    outs, rows_refs, sems = rest[-3 * STREAMS - 1 : -STREAMS - 1], rest[-STREAMS - 1 : -1], rest[-1]
    copies = []
    for s, order in enumerate(orders):
        count, width = halves[s].shape[0], halves[s].shape[2]
        rows = halves[s].shape[1] // STREAMS
        for q in range(count):
            for c in range(STREAMS):
                value = halves[s][q, c * rows : (c + 1) * rows].astype(F32)
                rows_refs[s][q, :, c * width : (c + 1) * width] = value
            device = me_ref[0] ^ places(order)[half_index * count + q]
            done = 0
            for p, (_, share) in enumerate(parts[s]):
                start = pl.multiple_of(device * share, 8)
                copy = pltpu.make_async_copy(
                    rows_refs[s].at[q, pl.ds(done, share)],
                    outs[2 * s + p].at[pl.ds(start, share)],
                    sems.at[len(copies)],
                )
                copy.start()
                copies.append(copy)
                done += share
    for copy in copies:
        copy.wait()


def unpack_whole(order, me_ref, near_ref, far_ref, first_ref, second_ref, total_ref):
    half, width = near_ref.shape[0], near_ref.shape[2]
    rows = near_ref.shape[1] // STREAMS
    for q, offset in enumerate(places(order)):
        ref, place = (near_ref, q) if q < half else (far_ref, q - half)
        start = pl.multiple_of((me_ref[0] ^ offset) * rows, 8)
        for s in range(STREAMS):
            value = ref[place, s * rows : (s + 1) * rows].astype(F32)
            total_ref[pl.ds(start, rows), s * width : (s + 1) * width] = value
    cut = first_ref.shape[0]
    first_ref[...] = total_ref[:cut]
    second_ref[...] = total_ref[cut : cut + second_ref.shape[0]]


def params(axes=0):
    return pltpu.CompilerParams(
        vmem_limit_bytes=VMEM_LIMIT,
        dimension_semantics=("arbitrary",) * axes if axes else None,
    )


def cost(flops, moved):
    return pl.CostEstimate(flops=flops, bytes_accessed=moved, transcendentals=0)


def whole(array_shape):
    return pl.BlockSpec(array_shape, lambda *_: (0,) * len(array_shape))


def struct(shape, dtype):
    return jax.ShapeDtypeStruct(shape, dtype)


def on_device(
    node_state,
    edge_state,
    edge_source,
    contact_block,
    contact_host,
    contact_remote,
    w_edge_in,
    w_edge_out,
    w_node_in,
    w_node_out,
    w_contact_in,
    w_contact_out,
    node_cot,
    edge_cot,
):
    node_count, latent = node_state.shape
    edge_count = edge_state.shape[0]
    groups = lax.axis_size("dom")
    blocks = node_count // BLOCK
    row_count = contact_block.shape[0]
    width = latent // STREAMS
    orders = exchange_orders(groups)
    me = lax.axis_index("dom").astype(jnp.int32).reshape(1)
    host = contact_host[:, 0]
    smem = pl.BlockSpec(memory_space=pltpu.SMEM)
    anywhere = pl.BlockSpec(memory_space=pl.ANY)

    inner, outer = swap_rims(node_state[:RIM], node_state[node_count - RIM :])
    last = len(orders[0]) - 1
    far_bit = orders[0][-1]
    half = groups // 2
    rows_named = jnp.concatenate([host, contact_remote])
    arrived, inner, outer, *named = joined(
        [swap(node_state, far_bit), inner, outer]
        + [swap(rows_named, order[0]) for order in orders[:2]]
    )
    before, after = sorted_rims(inner, outer)
    pair = jnp.stack([node_state, arrived])
    slabs = [pair[:, :, s * width : (s + 1) * width] for s in range(STREAMS)]
    for step in range(1, last):
        if step == last - 1:
            *slabs, before, rows_named = joined([*slabs, before, rows_named])
            named.append(swap(rows_named, orders[2][0]))
        arrived = gather_step(slabs, orders, step)
        if step < last - 1:
            slabs = both(slabs, joined(arrived))

    steps = edge_count // EDGE_ROWS
    sources = edge_source.reshape(steps, 1, EDGE_ROWS)
    edge_block = pl.BlockSpec((EDGE_ROWS, latent), lambda i: (i, 0))
    node_block = pl.BlockSpec((EDGE_ROWS // EPN, latent), lambda i: (i, 0))
    source_block = pl.BlockSpec((1, 1, EDGE_ROWS), lambda i: (i, 0, 0))
    rim_block = whole((RIM, latent))
    extended_rows = node_count + 2 * RIM
    edge_out, mesh_sum, e_pre, e_linear = pl.pallas_call(
        edge_forward,
        grid=(steps,),
        in_specs=[
            source_block,
            rim_block,
            whole(node_state.shape),
            rim_block,
            edge_block,
            whole(w_edge_in.shape),
            whole(w_edge_out.shape),
        ],
        out_specs=[edge_block, node_block, edge_block, edge_block],
        out_shape=[
            struct((edge_count, latent), BF16),
            struct((node_count, latent), BF16),
            struct((edge_count, latent), F32),
            struct((edge_count, latent), F32),
        ],
        scratch_shapes=[
            pltpu.VMEM((extended_rows, latent), BF16),
            pltpu.VMEM((EDGE_ROWS, 3 * latent), BF16),
            pltpu.VMEM((EDGE_ROWS, latent), BF16),
        ],
        compiler_params=params(1),
        cost_estimate=cost(2 * edge_count * latent * latent * 6, edge_count * latent * 16),
        name="edge_forward",
    )(sources, before, node_state, after, edge_state, w_edge_in, w_edge_out)

    *arrived, named[2], mesh_sum = joined([*arrived, named[2], mesh_sum])
    quarters = [
        value.reshape(half * blocks // 2, BLOCK, width)
        for pair in zip(slabs, arrived)
        for value in pair
    ]
    picked = pl.pallas_call(
        functools.partial(pick_blocks, orders, blocks, row_count),
        in_specs=[smem] * (1 + STREAMS) + [anywhere] * (2 * STREAMS),
        out_specs=[anywhere] * STREAMS,
        out_shape=[struct((row_count, BLOCK, width), BF16)] * STREAMS,
        scratch_shapes=[pltpu.SemaphoreType.DMA((STREAMS * row_count,))],
        compiler_params=params(),
        cost_estimate=cost(0, 2**20),
        name="pick_blocks",
    )(me, *named, *quarters)
    joined_now = joined([*picked, *quarters])
    picked, quarters = joined_now[:STREAMS], joined_now[STREAMS:]
    slabs = [jnp.concatenate(quarters[2 * s : 2 * s + 2], axis=0) for s in range(STREAMS)]
    answered = [swap(value, order[0]) for value, order in zip(picked, orders)]

    def near_spec(row, s):
        def index(i, me_ref, host_ref, remote_ref, block_ref):
            spot = place_of(orders[s], host_ref[row] ^ me_ref[0])
            return (jnp.where(spot < half, spot * blocks + remote_ref[row], 0), 0, 0)

        return pl.BlockSpec((1, BLOCK, width), index)

    def answer_spec(row):
        return pl.BlockSpec((1, BLOCK, width), lambda *_: (row, 0, 0))

    far = []
    for row in range(row_count):
        for s in range(STREAMS):
            far += [(near_spec(row, s), slabs[s]), (answer_spec(row), answered[s])]
    far_specs, far_args = [spec for spec, _ in far], [arg for _, arg in far]
    matrices = [(w_edge_in, w_edge_out), (w_node_in, w_node_out), (w_contact_in, w_contact_out)]
    parts = [parts_of(first.shape[0], second.shape[0], groups) for first, second in matrices]
    pair_rows = [chunk_rows(part) for part in parts]
    halves = lambda rows: [struct((half, rows * STREAMS, width), BF16)] * 2
    remote_parts = [
        struct((row_count, BLOCK, columns), BF16) for columns in (2 * width, latent - 2 * width)
    ]
    b_out = [
        struct((node_count, latent), BF16),
        struct((node_count, latent), F32),
        struct((node_count, latent), BF16),
        *halves(pair_rows[1]),
        *halves(pair_rows[2]),
        *remote_parts,
    ]
    b_args = [node_state, mesh_sum, node_cot, w_node_in, w_node_out, w_contact_in, w_contact_out]
    contact_rows = row_count * BLOCK
    chunk_length = min(4, row_count) * BLOCK
    (node_out, partial_h, d_mesh, n_kept, n_sent, c_kept, c_sent, *away) = pl.pallas_call(
        functools.partial(node_and_contact, orders, parts[1], parts[2], row_count),
        grid_spec=pltpu.PrefetchScalarGridSpec(
            num_scalar_prefetch=4,
            grid=(1,),
            in_specs=far_specs
            + [anywhere if 3 <= i <= 4 else whole(arg.shape) for i, arg in enumerate(b_args)],
            out_specs=[
                anywhere if 3 <= i <= 4 else whole(out.shape) for i, out in enumerate(b_out)
            ],
            scratch_shapes=[
                pltpu.VMEM((contact_rows, 2 * latent), BF16),
                pltpu.VMEM((contact_rows, latent), F32),
                pltpu.VMEM((contact_rows, latent), F32),
                pltpu.VMEM((node_count, latent), F32),
                pltpu.VMEM((max(total_rows(part, groups) for part in parts[1:]), latent), F32),
                pltpu.VMEM((node_count, 3 * latent), BF16),
                pltpu.VMEM((node_count, latent), F32),
                pltpu.VMEM((chunk_length, 2 * latent), F32),
                pltpu.VMEM(w_node_in.shape, BF16),
                pltpu.VMEM(w_node_out.shape, BF16),
                pltpu.VMEM(b_out[3].shape, BF16),
                pltpu.VMEM(b_out[4].shape, BF16),
                pltpu.SemaphoreType.DMA((4,)),
            ],
        ),
        out_shape=b_out,
        compiler_params=params(1),
        cost_estimate=cost(2 * (contact_rows * 9 + node_count * 12) * latent * latent, 12 * 2**20),
        name="node_and_contact",
    )(me, host, contact_remote, contact_block, *far_args, *b_args)

    back = return_orders(orders)
    away_arrived = [swap(value, order[0]) for value, order in zip(away, back[1:])]
    n_arrived, c_arrived = swap(n_sent, orders[1][0]), swap(c_sent, orders[2][0])

    edge_grad, near_h, low, high, e_kept, e_sent = pl.pallas_call(
        functools.partial(edge_backward, orders, parts[0]),
        grid=(steps,),
        in_specs=[
            smem,
            source_block,
            rim_block,
            whole(node_state.shape),
            rim_block,
            edge_block,
            edge_block,
            edge_block,
            edge_block,
            node_block,
            whole((node_count, latent)),
            whole(w_edge_in.shape),
            whole(w_edge_out.shape),
        ],
        out_specs=[
            edge_block,
            whole((node_count, latent)),
            rim_block,
            rim_block,
            *[whole((half, pair_rows[0] * STREAMS, width))] * 2,
        ],
        out_shape=[
            struct((edge_count, latent), BF16),
            struct((node_count, latent), F32),
            struct((RIM, latent), BF16),
            struct((RIM, latent), BF16),
            *halves(pair_rows[0]),
        ],
        scratch_shapes=[
            pltpu.VMEM((extended_rows, latent), BF16),
            pltpu.VMEM((extended_rows, latent), F32),
            pltpu.VMEM((node_count, latent), F32),
            pltpu.VMEM((total_rows(parts[0], groups), latent), F32),
        ],
        compiler_params=params(1),
        cost_estimate=cost(2 * edge_count * latent * latent * 8, edge_count * latent * 20),
        name="edge_backward",
    )(me, sources, before, node_state, after, edge_state, e_pre, e_linear, edge_cot, d_mesh,
      partial_h, w_edge_in, w_edge_out)

    away_arrived[0], e_sent = joined([away_arrived[0], e_sent])
    e_arrived = swap(e_sent, orders[0][0])
    slots = half * blocks // 2
    placed = pl.pallas_call(
        functools.partial(add_to_places, back, blocks),
        in_specs=[smem] * 5 + [pl.BlockSpec(memory_space=pltpu.VMEM)] * 4,
        out_specs=[pl.BlockSpec(memory_space=pltpu.VMEM)] * (2 * STREAMS),
        out_shape=[
            struct((slots, BLOCK, width), dtype) for dtype in (F32, BF16) for _ in range(STREAMS)
        ],
        compiler_params=params(),
        cost_estimate=cost(0, 6 * 2**20),
        name="add_to_places",
    )(me, host, contact_remote, *named[:2], *away, *away_arrived)
    away_kept = placed[:STREAMS]
    n_arrived, c_arrived, *away_sent = joined([n_arrived, c_arrived, *placed[STREAMS:]])
    arrived = [swap(sent, order[1]) for sent, order in zip(away_sent, back)]
    *arrived, e_arrived = joined([*arrived, e_arrived])
    away = list(zip(away_kept, away_sent))
    away = added(away, arrived)
    weights = added(
        [(e_kept, e_sent), (n_kept, n_sent), (c_kept, c_sent)], [e_arrived, n_arrived, c_arrived]
    )
    for step in range(1, last - 1):
        sent = [jnp.concatenate([a[1], w[1]], axis=1) for a, w in zip(away, weights)]
        arrived = joined([swap(value, order[step]) for value, order in zip(sent, orders)])
        away = added(away, [value[:, :BLOCK] for value in arrived])
        weights = added(weights, [value[:, BLOCK:] for value in arrived])
    arrived = joined([swap(w[1], order[last - 1]) for w, order in zip(weights, orders)])
    mine = jnp.concatenate(
        [(w[0] + value.astype(F32)).astype(BF16) for w, value in zip(weights, arrived)], axis=1
    )
    mine, low, high = joined([mine, low, high])
    theirs, *rims = joined([swap(mine, far_bit), *swap_rims(low, high)])
    high, low = sorted_rims(*rims)
    pair = (mine.astype(F32) + theirs[::-1].astype(F32)).astype(BF16)
    cuts = [sum(pair_rows[:s]) * STREAMS for s in range(STREAMS + 1)]
    sums = [pair[:, cuts[s] : cuts[s + 1]] for s in range(STREAMS)]
    for step in range(1, last):
        sums = both(sums, joined(gather_step(sums, orders, step)))
    away_sent = jnp.concatenate([sent for _, sent in away], axis=2)
    *sums, away_sent = joined([*sums, away_sent])
    gathered = list(zip(sums, gather_step(sums, orders, last)))
    returned = swap(away_sent, far_bit)
    kept = jnp.concatenate([kept for kept, _ in away], axis=2)
    returned = (kept + returned.astype(F32)).reshape(node_count, latent)
    vmem = pl.BlockSpec(memory_space=pltpu.VMEM)
    if all(len(part) == 2 for part in parts):
        summed = []
        for side in range(2):
            summed = pl.pallas_call(
                functools.partial(unpack, orders, parts, side),
                in_specs=[smem] + [vmem] * STREAMS + [anywhere] * len(summed),
                out_specs=[anywhere] * (2 * STREAMS),
                out_shape=[struct(w.shape, F32) for pair in matrices for w in pair],
                scratch_shapes=[
                    *[pltpu.VMEM((half, rows, latent), F32) for rows in pair_rows],
                    pltpu.SemaphoreType.DMA((2 * STREAMS * half,)),
                ],
                input_output_aliases={1 + STREAMS + i: i for i in range(len(summed))},
                compiler_params=params(),
                cost_estimate=cost(0, half * sum(pair_rows) * latent * 10),
                name="unpack",
            )(me, *[pair[side] for pair in gathered], *summed)
    else:
        summed = []
        for s, (first, second) in enumerate(matrices):
            summed += pl.pallas_call(
                functools.partial(unpack_whole, orders[s]),
                in_specs=[smem] + [vmem] * 2,
                out_specs=[vmem] * 2,
                out_shape=[struct(first.shape, F32), struct(second.shape, F32)],
                scratch_shapes=[pltpu.VMEM((pair_rows[s] * groups, latent), F32)],
                compiler_params=params(),
                name="unpack_whole",
            )(me, *gathered[s])

    rims = jnp.concatenate(
        [
            high.astype(F32),
            jnp.zeros((node_count - 2 * RIM, latent), F32),
            low.astype(F32),
        ],
        axis=0,
    )
    node_grad = (near_h + rims + returned).astype(BF16)
    return (node_out, edge_out, node_grad, edge_grad, *summed)


def solution(mesh):
    rows = P(("rep", "dom"), None)
    flat = P(("rep", "dom"))
    weight = P("rep", None)
    in_specs = (rows, rows, flat, flat, rows, flat) + (weight,) * 6 + (rows, rows)
    out_specs = (rows,) * 4 + (weight,) * 6
    return jax.shard_map(
        on_device, mesh=mesh, in_specs=in_specs, out_specs=out_specs, check_vma=False
    )
```
